128 devices in a mesh: gy: 4 (over z_hi, core), gz: 32 (over x, z_lo, y).
Axes of the slice: x: 4, y: 4, z: 4 (z_hi: 2, z_lo: 2; z = z_hi * 2 + z_lo), core: 2. Of those that a mesh axis runs over, the one named last changes fastest.
Arguments:
- velocity_hat: float32 [3, 2, 256, 256, 128], P(None, None, 'gy', 'gz'), may hold values from -3 to 3
- inflow: float32 [3], replicated, may hold values from -0.4 to 1.2, as said below
- viscosity: float32 [128, 256, 512], P('gz', 'gy'), may hold values from 0.03 to 0.3
- cot_hat: float32 [3, 2, 256, 256, 128], P(None, None, 'gy', 'gz'), may hold values from -6 to 6
- mode_mask: int32 [256, 256, 128], P('gy', 'gz'), may hold values from 0 to 1, as said below
- hub_cells: int32 [100, 3], replicated, may hold values from 0 to 511, as said below
- yaw_sector: int32 [100], replicated, may hold values from 0 to 12
- thrust: float32 [100], replicated, may hold values from 0.5 to 2
Outputs:
- adjoint_hat: float32 [3, 2, 256, 256, 128], P(None, None, 'gy', 'gz')
- thrust_grad: float32 [100], replicated
The draws below stay inside these ranges and needn't reach their ends.
Inputs may be any that keep to these rules, and one draw needn't show every extreme that they name: `mode_mask`: 1 exactly at the modes with kx < cx, |my| < cy and |mz| < cz, where the cutoffs are drawn anew between a quarter and a third of 512, 256 and 128; 0 elsewhere. `hub_cells`: row t holds the x, y and z cells of turbine t's hub; every disk of radius 4 in the y-z plane lies inside the grid, and no two disks share a cell. `inflow`: x component within 0.8 to 1.2, y within -0.4 to 0.4, z within -0.2 to 0.2.
All inputs are finite; a program needn't handle non-finite values.
Results may differ from the reference program's by a relative error of at most 0.00013.
Values sent between devices are 32-bit elements; how exact they have to be, the bound alone decides.
A program may use at most 128 MiB of HBM per device.

```python
import math
import jax
import jax.numpy as jnp
from jax import lax

NX = 512
NY = 256
NZ = 128
TURBINES = 100
KX = 256
RADIUS = 4


def draw_inflow(key, part):
    key = jax.random.fold_in(key, 37)
    lower = jnp.array([0.8, -0.4, -0.2], jnp.float32)
    upper = jnp.array([1.2, 0.4, 0.2], jnp.float32)
    return lower + (upper - lower) * jax.random.uniform(key, (3,), jnp.float32)


def draw_mode_mask(key, part):
    key = jax.random.fold_in(key, 11)
    subkeys = jax.random.split(key, 3)
    cut_x = jax.random.randint(subkeys[0], (), NX // 4, NX // 3 + 1)
    cut_y = jax.random.randint(subkeys[1], (), NY // 4, NY // 3 + 1)
    cut_z = jax.random.randint(subkeys[2], (), NZ // 4, NZ // 3 + 1)
    index_x = jnp.arange(KX, dtype=jnp.int32)
    index_y = jnp.arange(NY, dtype=jnp.int32)
    index_z = jnp.arange(NZ, dtype=jnp.int32)
    signed_y = jnp.abs(jnp.where(index_y < NY // 2, index_y, index_y - NY))
    signed_z = jnp.abs(jnp.where(index_z < NZ // 2, index_z, index_z - NZ))
    inside = (index_x < cut_x)[:, None, None] & (signed_y < cut_y)[None, :, None] & (signed_z < cut_z)[None, None, :]
    return inside.astype(jnp.int32)


def draw_hub_cells(key, part):
    key = jax.random.fold_in(key, 23)
    subkeys = jax.random.split(key, 3)
    turbine = jnp.arange(TURBINES, dtype=jnp.int32)
    row_index = turbine // 10
    col_index = turbine % 10
    jitter_y = NY // 80
    cell_x = row_index * NX // 10 + jax.random.randint(subkeys[0], (TURBINES,), 0, NX // 20 + 1)
    cell_y = col_index * NY // 10 + NY // 20 + jax.random.randint(subkeys[1], (TURBINES,), -jitter_y, jitter_y + 1)
    cell_z = NZ // 4 + jax.random.randint(subkeys[2], (TURBINES,), -1, 2)
    return jnp.stack([cell_x, cell_y, cell_z], axis=1).astype(jnp.int32)


def with_ends(values, own_key, low, high):
    shape = values.shape
    index_at = [jax.random.randint(jax.random.fold_in(own_key, axis), (), 0, shape[axis]) for axis in range(len(shape))]
    values = values.at[tuple(index_at)].set(low)
    longest = shape.index(max(shape))
    index_at[longest] = (index_at[longest] + 1) % shape[longest]
    return values.at[tuple(index_at)].set(high)


def steps_of(own_key, extent, cuts, least, high):
    gain = 1.0
    for position, shards_of in cuts:
        steps = jax.random.uniform(jax.random.fold_in(jax.random.fold_in(own_key, 6), position), (shards_of,), jnp.float32, least / len(cuts), high / len(cuts))
        gain = gain * jnp.repeat(jnp.exp(steps), extent[position] // shards_of).reshape((-1,) + (1,) * (len(extent) - 1 - position))
    return gain


def centred(rng, shape, width, bound, cuts=(), held_as=jnp.bfloat16):
    loudness = steps_of(rng, shape, cuts, -0.22, 0.18) if cuts else 1.0
    entries = jax.random.normal(rng, shape, jnp.float32) * width * loudness
    return jnp.minimum(jnp.maximum(entries, -bound), bound).astype(held_as)


def setup_inputs(seed: int = 0) -> dict:
    seeds = jax.random.split(jax.random.key(seed), 9)
    return {
        "velocity_hat": centred(seeds[0], (3, 2, KX, NY, NZ), 0.5, 3.0, ((2, 4), (3, 32)), jnp.float32),
        "inflow": draw_inflow(jax.random.fold_in(seeds[8], 71), 0),
        "viscosity": jnp.clip(jnp.exp(math.log(0.3) - 2.3025852 * jax.random.uniform(seeds[2], (NZ, NY, NX), jnp.float32) ** steps_of(seeds[2], (NZ, NY, NX), ((0, 32), (1, 4)), -0.2, 0.2)), 0.03, 0.3),
        "cot_hat": centred(seeds[3], (3, 2, KX, NY, NZ), 1.0, 6.0, ((2, 4), (3, 32)), jnp.float32),
        "mode_mask": draw_mode_mask(jax.random.fold_in(seeds[8], 71), 0),
        "hub_cells": draw_hub_cells(jax.random.fold_in(seeds[8], 71), 0),
        "yaw_sector": with_ends(jax.random.randint(seeds[6], (TURBINES,), 0, 13), jax.random.fold_in(seeds[6], 1), 0, 12).astype(jnp.int32),
        "thrust": jnp.clip(jnp.exp(jax.random.uniform(seeds[7], (TURBINES,), jnp.float32, math.log(0.5), math.log(2.0))), 0.5, 2.0),
    }


SECTION_STEP = 0.24
PRECISE = lax.Precision.HIGHEST

def signed_modes(index, length):
    return jnp.where(index < length // 2, index, index - length)

def wave_vectors():
    wave_x = 2.0 * math.pi / NX * jnp.arange(KX, dtype=jnp.int32).astype(jnp.float32)
    wave_y = 2.0 * math.pi / NY * signed_modes(jnp.arange(NY, dtype=jnp.int32), NY).astype(jnp.float32)
    wave_z = 2.0 * math.pi / NZ * signed_modes(jnp.arange(NZ, dtype=jnp.int32), NZ).astype(jnp.float32)
    return (wave_x[:, None, None], wave_y[None, :, None], wave_z[None, None, :])

def to_physical(modes):
    ordered = jnp.transpose(modes, (0, 3, 2, 1))
    padded = jnp.pad(ordered, ((0, 0), (0, 0), (0, 0), (0, 1)))
    return jnp.fft.irfftn(padded, s=(NZ, NY, NX), axes=(1, 2, 3), norm='ortho')

def to_modes(field):
    spectrum = jnp.fft.rfftn(field, axes=(1, 2, 3), norm='ortho')[:, :, :, :KX]
    return jnp.transpose(spectrum, (0, 3, 2, 1))

def curl_modes(modes, waves):
    wave_x, wave_y, wave_z = waves
    return 1j * jnp.stack([wave_y * modes[2] - wave_z * modes[1], wave_z * modes[0] - wave_x * modes[2], wave_x * modes[1] - wave_y * modes[0]])

def project_modes(modes, waves):
    wave_x, wave_y, wave_z = waves
    square = wave_x * wave_x + wave_y * wave_y + wave_z * wave_z
    inverse = (square > 0).astype(jnp.float32) / (square + (square == 0).astype(jnp.float32))
    along = (wave_x * modes[0] + wave_y * modes[1] + wave_z * modes[2]) * inverse
    return jnp.stack([modes[0] - wave_x * along, modes[1] - wave_y * along, modes[2] - wave_z * along])

def cross(first, second):
    return jnp.stack([first[1] * second[2] - first[2] * second[1], first[2] * second[0] - first[0] * second[2], first[0] * second[1] - first[1] * second[0]])

def disk_area():
    return float(sum((1 for offset_a in range(-RADIUS, RADIUS + 1) for offset_b in range(-RADIUS, RADIUS + 1) if offset_a * offset_a + offset_b * offset_b <= RADIUS * RADIUS)))

def turbine_frames(hub_cells, yaw_sector):
    angle = (yaw_sector.astype(jnp.float32) - 6.0) * (math.pi / 36.0)
    normal = jnp.stack([jnp.cos(angle), jnp.sin(angle), jnp.zeros_like(angle)], axis=1)
    along_x = (jnp.arange(NX, dtype=jnp.int32)[None, :] == hub_cells[:, 0:1]).astype(jnp.float32)
    offset_z = jnp.arange(NZ, dtype=jnp.int32)[None, :, None] - hub_cells[:, 2][:, None, None]
    offset_y = jnp.arange(NY, dtype=jnp.int32)[None, None, :] - hub_cells[:, 1][:, None, None]
    disk = (offset_z * offset_z + offset_y * offset_y <= RADIUS * RADIUS).astype(jnp.float32)
    return (normal, along_x, disk.reshape(disk.shape[0], NZ * NY))

def disk_project(field, normal, along_x, disk):
    flat = field.reshape(3, disk.shape[1], field.shape[-1])
    columns = jnp.einsum('cpx,tx->ctp', flat, along_x, precision=PRECISE)
    return jnp.einsum('ctp,tp,tc->t', columns, disk, normal, precision=PRECISE)

def spread(weights, normal, along_x, disk, shape):
    mixed = weights[:, None, None] * normal[:, :, None] * disk[:, None, :]
    return jnp.einsum('tcp,tx->cpx', mixed, along_x, precision=PRECISE).reshape(shape)

def advance(velocity_hat, thrust, inflow, viscosity, mode_mask, hub_cells, yaw_sector):
    waves = wave_vectors()
    modes = velocity_hat[:, 0] + 1j * velocity_hat[:, 1]
    velocity = to_physical(modes) + inflow[:, None, None, None]
    vorticity = to_physical(curl_modes(modes, waves))
    normal, along_x, disk = turbine_frames(hub_cells, yaw_sector)
    disk_speed = disk_project(velocity, normal, along_x, disk) / disk_area()
    force = spread(-0.5 * thrust * disk_speed * jnp.abs(disk_speed), normal, along_x, disk, velocity.shape)
    tendency = to_modes(cross(velocity, vorticity) + force) - curl_modes(to_modes(viscosity[None] * vorticity), waves)
    updated = mode_mask.astype(jnp.float32)[None] * project_modes(modes + SECTION_STEP * tendency, waves)
    return jnp.stack([jnp.real(updated), jnp.imag(updated)], axis=1)

def reference(velocity_hat, inflow, viscosity, cot_hat, mode_mask, hub_cells, yaw_sector, thrust):

    def forward(modes_in, thrust_in):
        return advance(modes_in, thrust_in, inflow, viscosity, mode_mask, hub_cells, yaw_sector)
    updated, pullback = jax.vjp(forward, velocity_hat, thrust)
    adjoint_hat, thrust_grad = pullback(cot_hat)
    return (adjoint_hat, thrust_grad)
```

```python
import math

import jax
import jax.numpy as jnp
import ml_dtypes
import numpy as np
from jax import lax
from jax.experimental import pallas as pl
from jax.experimental.pallas import tpu as pltpu
from jax.sharding import PartitionSpec as P

MESH = pl.DeviceIdType.MESH
F32 = jnp.float32
BF16 = jnp.bfloat16
RADIUS = 4
SECTION_STEP = 0.24
NX, NY, NZ = 512, 256, 128
WIDTH = 64
RING, RINGS = 8, 16


def disk_area():
    reach = range(-RADIUS, RADIUS + 1)
    return float(sum(1 for a in reach for b in reach if a * a + b * b <= RADIUS * RADIUS))


def signed(index, length):
    return np.where(index < length // 2, index, index - length)


def split(table):
    high = table.astype(ml_dtypes.bfloat16)
    low = (table - high.astype(np.float64)).astype(ml_dtypes.bfloat16)
    return np.stack([high, low])


def tables():
    e, w = np.meshgrid(np.arange(RING), np.arange(RINGS), indexing="ij")
    cell_z = ((w // 4) * 32 + (e // 4) * 16 + (w % 4) * 4 + e % 4).reshape(-1)
    mode_z = np.arange(NZ)
    wave_z = 2.0 * math.pi / NZ * signed(mode_z, NZ)
    angle = 2.0 * math.pi / NZ * (cell_z[:, None] * mode_z[None, :] % NZ)
    cos, sin = np.cos(angle), np.sin(angle)
    z_inverse = np.block([[cos, sin], [-wave_z * sin, wave_z * cos]])
    cos, sin = cos.T, sin.T
    wave_z = wave_z[:, None]
    z_first = np.block([cos, -sin, -wave_z * sin, -wave_z * cos])
    z_second = np.block([cos, -sin, wave_z * sin, wave_z * cos])
    row = np.arange(NY)
    w, z_lo, r = row // 16, row // 8 % 2, row % 8
    mode_y = (w // 4) * 64 + z_lo * 32 + (w % 4) * 8 + r
    angle = 2.0 * math.pi / NY * (np.arange(NY)[:, None] * mode_y[None, :] % NY)
    cos, sin = np.cos(angle), np.sin(angle)
    y_inverse = np.concatenate([cos, sin])
    y_forward = np.concatenate([cos.T, sin.T])
    lane = np.arange(NX)
    mode_x = lane // 128 * WIDTH + lane % WIDTH
    weight = np.where(mode_x == 0, 1.0, 2.0) / math.sqrt(NX * NY * NZ)
    angle = 2.0 * math.pi / NX * (mode_x[:, None] * np.arange(NX)[None, :] % NX)
    real = (lane % 128 < WIDTH)[:, None]
    x_inverse = weight[:, None] * np.where(real, np.cos(angle), -np.sin(angle))
    return [split(t) for t in (z_inverse, np.stack([z_first, z_second]), y_inverse, y_forward, x_inverse, x_inverse.T)]


def halves(value):
    high = value.astype(BF16)
    return high, (value - high.astype(F32)).astype(BF16)


def dot(left, right):
    return jnp.dot(left, right, preferred_element_type=F32)


def dot_nt(left, right):
    return lax.dot_general(left, right, (((1,), (1,)), ((), ())), preferred_element_type=F32)


def three(left, right, product=dot):
    return product(left[0], right[0]) + product(left[0], right[1]) + product(left[1], right[0])


def kernel(
    modes_ref, inflow_ref, visc_ref, cot_ref, mask_ref, turb_ref,
    zi_ref, zf_ref, yi_ref, yf_ref, xi_ref, xf_ref,
    out_ref, grad_ref,
    adj, sent, ring, plane, phys, visc, rows, back, fold, pencil, part, part_a, part_b,
    s1, r1, s2, r2, s3, r3, s4, r4, sv, rv, sa, ra,
):
    gy = lax.axis_index("gy")
    gz = lax.axis_index("gz")
    x = gz // 8
    z_lo = gz // 4 % 2
    y = gz % 4
    e = z_lo * 4 + gy
    w = x * 4 + y

    def ring_id(other):
        return {"gy": other % 4, "gz": x * 8 + other // 4 * 4 + y}

    def sheet_id(other):
        return {"gy": gy, "gz": other // 4 * 8 + z_lo * 4 + other % 4}

    def to_ring(step):
        return (e + step) % RING

    def to_sheet(step):
        return (w + step) % RINGS

    barrier = pltpu.get_barrier_semaphore()

    @pl.loop(1, RING)
    def _(step):
        pl.semaphore_signal(barrier, inc=1, device_id=ring_id(to_ring(step)), device_id_type=MESH)

    @pl.loop(1, RINGS)
    def _(step):
        pl.semaphore_signal(barrier, inc=1, device_id=sheet_id(to_sheet(step)), device_id_type=MESH)

    pl.semaphore_wait(barrier, RING + RINGS - 2)

    def exchange(steps, target, device, source, landing, send, receive):
        @pl.loop(1, steps)
        def _(step):
            other = target(step)
            pltpu.make_async_remote_copy(
                src_ref=source(other), dst_ref=landing, send_sem=send, recv_sem=receive,
                device_id=device(other), device_id_type=MESH,
            ).start()

        pltpu.make_async_copy(source(target(0)), landing, receive).start()

    def drain(ref, sem):
        pltpu.make_async_copy(ref, ref, sem).wait()

    def lanes(index):
        return pl.ds(pl.multiple_of(index * 128, 128), 128)

    def octet(index):
        return pl.ds(pl.multiple_of(index * 8, 8), 8)

    def send_visc():
        landing = visc.at[pl.ds(pl.multiple_of(gy * 64, 64), 64)]

        @pl.loop(1, 4)
        def _(step):
            other = (gy + step) % 4
            pltpu.make_async_remote_copy(
                src_ref=visc_ref.at[other], dst_ref=landing, send_sem=sv.at[0], recv_sem=rv.at[0],
                device_id={"gy": other, "gz": gz}, device_id_type=MESH,
            ).start()

        pltpu.make_async_copy(visc_ref.at[gy], landing, rv.at[0]).start()

    def send_ring(f):
        exchange(
            RING, to_ring, ring_id, lambda k: sent.at[f, k],
            ring.at[f, :, octet(z_lo), lanes(gy)], s1.at[f], r1.at[f],
        )

    def send_sheet(f):
        drain(ring.at[f], r1.at[f])
        slot = jnp.where(f < 5, f, f + 1)
        exchange(
            RINGS, to_sheet, sheet_id, lambda k: ring.at[f, k],
            plane.at[slot, w], s2.at[f], r2.at[f],
        )

    def z_inverse(source, f, base):
        table = (zi_ref[0], zi_ref[1])
        view = sent.reshape(10, 1024, 128)
        for pair in range(4):
            wide = []
            for ky in (2 * pair, 2 * pair + 1):
                own = source[f, pl.ds(ky, 128, stride=8), :]
                wide.append(jnp.concatenate([own, jnp.concatenate([-own[64:], own[:64]], 0)], 1))
            done = three(table, halves(jnp.concatenate(wide, 0)), dot_nt)
            for k in range(2):
                at = pl.ds(2 * pair + k, 128, stride=8)
                view[base + f, at, :] = done[:128, k * 128 : k * 128 + 128]

                @pl.when(f < 2)
                def _():
                    view[base + 3 + f, at, :] = done[128:, k * 128 : k * 128 + 128]

    def z_fields(source, base):
        @pl.loop(0, 3)
        def _(f):
            z_inverse(source, f, base)
            send_ring(base + f)

            @pl.when(f < 2)
            def _():
                send_ring(base + 3 + f)

    z_fields(modes_ref, 0)
    send_visc()

    def tile_waves(kx):
        wave_x = (2.0 * math.pi / NX) * (gy * WIDTH + kx).astype(F32)
        iy = gz * 8 + lax.broadcasted_iota(jnp.int32, (8, 128), 0)
        iz = lax.broadcasted_iota(jnp.int32, (8, 128), 1)
        wave_y = (2.0 * math.pi / NY) * jnp.where(iy < NY // 2, iy, iy - NY).astype(F32)
        wave_z = (2.0 * math.pi / NZ) * jnp.where(iz < NZ // 2, iz, iz - NZ).astype(F32)
        return wave_x, wave_y, wave_z

    @pl.loop(0, WIDTH)
    def _(kx):
        wave_x, wave_y, wave_z = tile_waves(kx)
        square = wave_x * wave_x + wave_y * wave_y + wave_z * wave_z
        inverse = jnp.where(square > 0, 1.0, 0.0) / jnp.where(square > 0, square, 1.0)
        first = octet(kx)
        scale = mask_ref[first, :].astype(F32) * jnp.where(gy * WIDTH + kx == 0, 1.0, 0.5)
        for c in range(2):
            at = octet(c * WIDTH + kx)
            v0, v1, v2 = cot_ref[0, at, :], cot_ref[1, at, :], cot_ref[2, at, :]
            along = (wave_x * v0 + wave_y * v1 + wave_z * v2) * inverse
            adj[0, at, :] = scale * (v0 - wave_x * along)
            adj[1, at, :] = scale * (v1 - wave_y * along)
            adj[2, at, :] = scale * (v2 - wave_z * along)

    z_fields(adj, 5)

    @pl.loop(0, 5)
    def _(f):
        send_sheet(f)

    lane = lax.broadcasted_iota(jnp.int32, (1, NX), 1)
    wave_x = (2.0 * math.pi / NX) * ((lane // 128) * WIDTH + lane % WIDTH).astype(F32)
    sign = jnp.where(lane % 128 < WIDTH, -1.0, 1.0).astype(F32)

    def turn(value):
        parts = [pltpu.roll(value[:, k * 128 : k * 128 + 128], 64, 1) for k in range(value.shape[1] // 128)]
        return jnp.concatenate(parts, 1) * sign[:, : value.shape[1]]

    def wave_y_of(block):
        row = lax.broadcasted_iota(jnp.int32, (16, 1), 0)
        mode = (block // 4) * 64 + (block % 4) * 8 + (row // 8) * 32 + row % 8
        return (2.0 * math.pi / NY) * jnp.where(mode < NY // 2, mode, mode - NY).astype(F32)

    def to_cells(group, j):
        index = group * 6 + j
        for h in range(2):
            cols = pl.ds(h * 256, 256)
            both = three((yi_ref[0], yi_ref[1]), halves(plane[index, :, :, cols].reshape(NY, 256)))
            rows[:, cols] = both[:NY] + turn(both[NY:])
        moved = halves(rows[...])
        for h in range(2):
            cols = pl.ds(h * 256, 256)
            done = three(moved, (xi_ref[0, :, cols], xi_ref[1, :, cols]))
            phys[index, :, cols] = done

    @pl.loop(0, 2)
    def _(group):
        @pl.loop(0, 5)
        def _(j):
            drain(plane.at[group * 6 + j], r2.at[group * 5 + j])

        base = group * 6

        @pl.loop(0, RINGS)
        def _(block):
            wave_y = wave_y_of(block)
            t0, t1, t2 = [turn(plane[base + k, block]) for k in range(3)]
            d0, d1 = plane[base + 3, block], plane[base + 4, block]
            plane[base + 3, block] = d0 - wave_x * t2
            plane[base + 4, block] = wave_y * t2 - d1
            plane[base + 5, block] = wave_x * t1 - wave_y * t0

        @pl.loop(0, 6)
        def _(j):
            to_cells(group, j)

            @pl.when((group == 0) & (j < 5))
            def _():
                send_sheet(5 + j)

    hub_x, hub_y, hub_z = turb_ref[0:1, :], turb_ref[1:2, :], turb_ref[2:3, :]
    normal_x, normal_y, thrust = turb_ref[3:4, :], turb_ref[4:5, :], turb_ref[5:6, :]
    cell_x = lax.broadcasted_iota(jnp.int32, (NX, 128), 0).astype(F32)
    hot = jnp.where(cell_x == hub_x, 1.0, 0.0).astype(BF16)
    off_y = lax.broadcasted_iota(jnp.int32, (NY, 128), 0).astype(F32) - hub_y
    off_z = (gz * 4 + gy).astype(F32) - hub_z
    disk = jnp.where(off_y * off_y + off_z * off_z <= float(RADIUS * RADIUS), 1.0, 0.0)

    def project(first, inflow):
        def column(index, mean):
            high, low = halves(phys[index] + mean)
            return dot(high, hot) + dot(low, hot)

        mixed = normal_x * column(first, inflow[0]) + normal_y * column(first + 1, inflow[1])
        return jnp.sum(disk * mixed, axis=0, keepdims=True)

    part[...] = jnp.zeros((8, 128), F32)
    part[0:1, :] = project(0, (inflow_ref[0], inflow_ref[1]))
    part[1:2, :] = project(6, (0.0, 0.0))
    exchange(RING, to_ring, ring_id, lambda k: part, part_a.at[e], sa.at[0], ra.at[0])
    drain(visc, rv.at[0])

    @pl.loop(0, 32)
    def _(block):
        at = octet(block)
        u0, u1, u2 = [phys[k, at] + inflow_ref[k] for k in range(3)]
        w1, w0, w2 = [phys[3 + k, at] for k in range(3)]
        p0, p1, p2 = [phys[6 + k, at] for k in range(3)]
        q1, q0, q2 = [phys[9 + k, at] for k in range(3)]
        nu = visc[at]
        phys[0, at] = p1 * u2 - p2 * u1 - nu * q0
        phys[1, at] = p2 * u0 - p0 * u2 - nu * q1
        phys[2, at] = p0 * u1 - p1 * u0 - nu * q2
        phys[3, at] = w1 * p2 - w2 * p1
        phys[4, at] = w2 * p0 - w0 * p2
        phys[5, at] = w0 * p1 - w1 * p0

    drain(part_a, ra.at[0])
    total = part_a[0]
    for k in range(1, RING):
        total = total + part_a[k]
    part_b[RINGS] = total
    exchange(RINGS, to_sheet, sheet_id, lambda k: part_b.at[RINGS], part_b.at[w], sa.at[1], ra.at[1])

    def add_force():
        drain(part_b.at[pl.ds(0, RINGS)], ra.at[1])
        total = part_b[0]
        for k in range(1, RINGS):
            total = total + part_b[k]
        disk_speed = total[0:1] / disk_area()
        push = total[1:2]
        grad_ref[...] = jnp.broadcast_to(-0.5 * SECTION_STEP * disk_speed * jnp.abs(disk_speed) * push, (8, 128))
        weight = -thrust * jnp.abs(disk_speed) * push / disk_area()
        for index, normal in ((3, normal_x), (4, normal_y)):
            high, low = halves(disk * (weight * normal))
            phys[index] = phys[index] + dot_nt(high, hot) + dot_nt(low, hot)

    def send_back(k):
        exchange(
            RINGS, to_sheet, sheet_id, lambda other: back.at[k, other],
            fold.at[k, w], s3.at[k], r3.at[k],
        )

    def send_home(k):
        drain(fold.at[k], r3.at[k])
        exchange(
            RING, to_ring, ring_id, lambda other: fold.at[k, :, octet(other // 4), lanes(other % 4)],
            pencil.at[k, e], s4.at[k], r4.at[k],
        )

    @pl.loop(0, 6)
    def _(j):
        @pl.when(j == 3)
        def _():
            add_force()

        moved = halves(phys[j])
        for h in range(2):
            cols = pl.ds(h * 256, 256)
            spectrum = three(moved, (xf_ref[0, :, cols], xf_ref[1, :, cols]))
            both = three((yf_ref[0], yf_ref[1]), halves(spectrum))
            plane[j, :, :, cols] = (both[:NY] - turn(both[NY:])).reshape(RINGS, 16, 256)

        @pl.loop(0, RINGS)
        def _(block):
            own = plane[j, block]

            @pl.when(j < 2)
            def _():
                back[j, block] = own

            @pl.when(j == 3)
            def _():
                back[2, block] = own + wave_y_of(block) * turn(plane[2, block])

            @pl.when(j == 4)
            def _():
                back[3, block] = own - wave_x * turn(plane[2, block])

            @pl.when(j == 5)
            def _():
                back[4, block] = own + wave_x * turn(plane[1, block]) - wave_y_of(block) * turn(plane[0, block])

        @pl.when(j < 2)
        def _():
            send_back(j)

        @pl.when(j > 2)
        def _():
            send_back(j - 1)

        @pl.when((j == 2) | (j == 3))
        def _():
            send_home(j - 2)

        @pl.when(j > 3)
        def _():
            send_home(j - 2)

    send_home(4)

    @pl.loop(0, 5)
    def _(k):
        drain(pencil.at[k], r4.at[k])

    pencils = pencil.reshape(5, 1024, 128)

    def z_forward(f, table, fields):
        for pair in range(4):
            tall = []
            for k in fields:
                own = jnp.concatenate([pencils[k, pl.ds(2 * pair + i, 128, stride=8), :] for i in range(2)], 1)
                tall += [own, turn(own)]
            done = three(table, halves(jnp.concatenate(tall, 0)))
            for i in range(2):
                at = pl.ds(2 * pair + i, 128, stride=8)
                doubled = jnp.where(
                    (lax.broadcasted_iota(jnp.int32, (128, 1), 0) % WIDTH == 0) & (gy == 0), 1.0, 2.0
                )
                out_ref[f, at, :] = adj[f, at, :] * doubled + SECTION_STEP * done[:, i * 128 : i * 128 + 128].T

    z_forward(0, (zf_ref[0, 0], zf_ref[1, 0]), (2, 1))
    z_forward(1, (zf_ref[0, 1], zf_ref[1, 1]), (3, 0))
    z_forward(2, (zf_ref[0, 0, :, :256], zf_ref[1, 0, :, :256]), (4,))

    @pl.loop(0, 10)
    def _(f):
        drain(sent.at[f, pl.ds(0, RING - 1)], s1.at[f])
        drain(ring.at[f, pl.ds(0, RINGS - 1)], s2.at[f])

    @pl.loop(0, 5)
    def _(k):
        drain(back.at[k, pl.ds(0, RINGS - 1)], s3.at[k])
        drain(pencil.at[k, pl.ds(0, RING - 1)], s4.at[k])

    drain(visc.at[pl.ds(0, 192)], sv.at[0])
    drain(part_a.at[pl.ds(0, RING - 1)], sa.at[0])
    drain(part_b.at[pl.ds(0, RINGS - 1)], sa.at[1])


def local(velocity_hat, inflow, viscosity, cot_hat, mode_mask, hub_cells, yaw_sector, thrust):
    count = thrust.shape[0]
    angle = (yaw_sector.astype(F32) - 6.0) * (math.pi / 36.0)
    hubs = hub_cells.astype(F32)
    turbines = jnp.stack([hubs[:, 0], hubs[:, 1], hubs[:, 2], jnp.cos(angle), jnp.sin(angle), thrust, thrust, thrust])
    turbines = jnp.pad(turbines, ((0, 0), (0, 128 - count)), constant_values=-1000.0)
    vmem = pl.BlockSpec(memory_space=pltpu.VMEM)
    smem = pl.BlockSpec(memory_space=pltpu.SMEM)
    dma = pltpu.SemaphoreType.DMA
    adjoint, grad = pl.pallas_call(
        kernel,
        out_shape=(
            jax.ShapeDtypeStruct((3, 1024, 128), F32),
            jax.ShapeDtypeStruct((8, 128), F32),
        ),
        in_specs=[vmem, smem] + [vmem] * 10,
        out_specs=(vmem, vmem),
        scratch_shapes=[
            pltpu.VMEM((3, 1024, 128), F32),
            pltpu.VMEM((10, RING, RINGS, 8, 128), F32),
            pltpu.VMEM((10, RINGS, 16, NX), F32),
            pltpu.VMEM((12, RINGS, 16, NX), F32),
            pltpu.VMEM((12, NY, NX), F32),
            pltpu.VMEM((NY, NX), F32),
            pltpu.VMEM((NY, NX), F32),
            pltpu.VMEM((5, RINGS, 16, NX), F32),
            pltpu.VMEM((5, RINGS, 16, NX), F32),
            pltpu.VMEM((5, RING, RINGS, 8, 128), F32),
            pltpu.VMEM((8, 128), F32),
            pltpu.VMEM((RING, 8, 128), F32),
            pltpu.VMEM((RINGS + 1, 8, 128), F32),
            dma((10,)), dma((10,)), dma((10,)), dma((10,)),
            dma((5,)), dma((5,)), dma((5,)), dma((5,)),
            dma((1,)), dma((1,)), dma((2,)), dma((2,)),
        ],
        compiler_params=pltpu.CompilerParams(
            collective_id=0, has_side_effects=True, vmem_limit_bytes=60 * 1024 * 1024
        ),
    )(
        velocity_hat.reshape(3, 1024, 128),
        inflow,
        viscosity,
        cot_hat.reshape(3, 1024, 128),
        mode_mask.reshape(512, 128),
        turbines,
        *[jnp.asarray(t) for t in tables()],
    )
    return adjoint.reshape(velocity_hat.shape), grad[0, :count]


def solution(mesh):
    placed = (
        P(None, None, "gy", "gz", None),
        P(),
        P("gz", "gy", None),
        P(None, None, "gy", "gz", None),
        P("gy", "gz", None),
        P(),
        P(),
        P(),
    )
    return jax.shard_map(
        local,
        mesh=mesh,
        in_specs=placed,
        out_specs=(P(None, None, "gy", "gz", None), P()),
        check_vma=False,
    )
```

```python
import math

import jax
import jax.numpy as jnp
import ml_dtypes
import numpy as np
from jax import lax
from jax.experimental import pallas as pl
from jax.experimental.pallas import tpu as pltpu
from jax.sharding import PartitionSpec as P

MESH = pl.DeviceIdType.MESH
F32 = jnp.float32
BF16 = jnp.bfloat16
RADIUS = 4
SECTION_STEP = 0.24
NX, NY, NZ = 512, 256, 128
WIDTH = 64
RING, RINGS = 8, 16


def disk_area():
    reach = range(-RADIUS, RADIUS + 1)
    return float(sum(1 for a in reach for b in reach if a * a + b * b <= RADIUS * RADIUS))


def signed(index, length):
    return np.where(index < length // 2, index, index - length)


def split(table):
    high = table.astype(ml_dtypes.bfloat16)
    low = (table - high.astype(np.float64)).astype(ml_dtypes.bfloat16)
    return np.stack([high, low])


def tables():
    e, w = np.meshgrid(np.arange(RING), np.arange(RINGS), indexing="ij")
    cell_z = ((w // 4) * 32 + (e // 4) * 16 + (w % 4) * 4 + e % 4).reshape(-1)
    mode_z = np.arange(NZ)
    wave_z = 2.0 * math.pi / NZ * signed(mode_z, NZ)
    angle = 2.0 * math.pi / NZ * (cell_z[:, None] * mode_z[None, :] % NZ)
    cos, sin = np.cos(angle), np.sin(angle)
    z_inverse = np.block([[cos, sin], [-wave_z * sin, wave_z * cos]])
    cos, sin = cos.T, sin.T
    wave_z = wave_z[:, None]
    z_first = np.block([cos, -sin, -wave_z * sin, -wave_z * cos])
    z_second = np.block([cos, -sin, wave_z * sin, wave_z * cos])
    row = np.arange(NY)
    w, z_lo, r = row // 16, row // 8 % 2, row % 8
    mode_y = (w // 4) * 64 + z_lo * 32 + (w % 4) * 8 + r
    angle = 2.0 * math.pi / NY * (np.arange(NY)[:, None] * mode_y[None, :] % NY)
    cos, sin = np.cos(angle), np.sin(angle)
    y_inverse = np.concatenate([cos, sin])
    y_forward = np.concatenate([cos.T, sin.T])
    lane = np.arange(NX)
    mode_x = lane // 128 * WIDTH + lane % WIDTH
    weight = np.where(mode_x == 0, 1.0, 2.0) / math.sqrt(NX * NY * NZ)
    angle = 2.0 * math.pi / NX * (mode_x[:, None] * np.arange(NX)[None, :] % NX)
    real = (lane % 128 < WIDTH)[:, None]
    x_inverse = weight[:, None] * np.where(real, np.cos(angle), -np.sin(angle))
    return [split(t) for t in (z_inverse, np.stack([z_first, z_second]), y_inverse, y_forward, x_inverse, x_inverse.T)]


def halves(value):
    high = value.astype(BF16)
    return high, (value - high.astype(F32)).astype(BF16)


def dot(left, right):
    return jnp.dot(left, right, preferred_element_type=F32)


def dot_nt(left, right):
    return lax.dot_general(left, right, (((1,), (1,)), ((), ())), preferred_element_type=F32)


def three(left, right, product=dot):
    return product(left[0], right[0]) + product(left[0], right[1]) + product(left[1], right[0])


def kernel(
    modes_ref, inflow_ref, visc_ref, cot_ref, mask_ref, turb_ref,
    zi_ref, zf_ref, yi_ref, yf_ref, xi_ref, xf_ref,
    out_ref, grad_ref,
    adj, sent, ring, sheet, plane, phys, visc, rows, fold, turned, pencil, part, part_a, part_b,
    s1, r1, s2, r2, s3, r3, s4, r4, sv, rv, sa, ra,
):
    gy = lax.axis_index("gy")
    gz = lax.axis_index("gz")
    x = gz // 8
    z_lo = gz // 4 % 2
    y = gz % 4
    z = gy // 2 * 2 + z_lo
    core = gy % 2
    e = z_lo * 4 + gy
    w = x * 4 + y
    kept_x = gy < 3
    kept = kept_x & ((gz < 11) | (gz > 20))

    def ring_id(other):
        return {"gy": other % 4, "gz": x * 8 + other // 4 * 4 + y}

    def sheet_id(other):
        return {"gy": gy, "gz": other // 4 * 8 + z_lo * 4 + other % 4}

    def to_ring(step):
        turn = step * 3 % RING
        there = (z + turn) % 4
        return there % 2 * 4 + there // 2 * 2 + (core + turn // 4) % 2

    def to_sheet(step):
        turn = step * 5 % RINGS
        return (x + turn // 4) % 4 * 4 + (y + turn) % 4

    barrier = pltpu.get_barrier_semaphore()

    @pl.loop(1, RING)
    def _(step):
        pl.semaphore_signal(barrier, inc=1, device_id=ring_id(to_ring(step)), device_id_type=MESH)

    @pl.loop(1, RINGS)
    def _(step):
        pl.semaphore_signal(barrier, inc=1, device_id=sheet_id(to_sheet(step)), device_id_type=MESH)

    pl.semaphore_wait(barrier, RING + RINGS - 2)

    def exchange(steps, target, device, source, landing, send, receive):
        @pl.loop(1, steps)
        def _(step):
            other = target(step)
            pltpu.make_async_remote_copy(
                src_ref=source(other), dst_ref=landing, send_sem=send, recv_sem=receive,
                device_id=device(other), device_id_type=MESH,
            ).start()

        pltpu.make_async_copy(source(target(0)), landing, receive).start()

    def to_rings(source, landing, send, receive):
        exchange(RING, to_ring, ring_id, source, landing, send, receive)

    def to_sheets(source, landing, send, receive):
        exchange(RINGS, to_sheet, sheet_id, source, landing, send, receive)

    def drain(ref, sem):
        pltpu.make_async_copy(ref, ref, sem).wait()

    tiles = sent.reshape(1280, 8, 128)

    def drain_tiles(count, sem):
        drain(tiles.at[pl.ds(0, count)], sem)

    def lanes(index):
        return pl.ds(pl.multiple_of(index * 128, 128), 128)

    def octet(index):
        return pl.ds(pl.multiple_of(index * 8, 8), 8)

    landing = visc.at[pl.ds(pl.multiple_of(gy * 64, 64), 64)]

    @pl.loop(1, 4)
    def _(step):
        other = (gy + step) % 4
        pltpu.make_async_remote_copy(
            src_ref=visc_ref.at[other], dst_ref=landing, send_sem=sv.at[0], recv_sem=rv.at[0],
            device_id={"gy": other, "gz": gz}, device_id_type=MESH,
        ).start()

    pltpu.make_async_copy(visc_ref.at[gy], landing, rv.at[0]).start()

    def tile_waves(kx):
        wave_x = (2.0 * math.pi / NX) * (gy * WIDTH + kx).astype(F32)
        iy = gz * 8 + lax.broadcasted_iota(jnp.int32, (8, 128), 0)
        iz = lax.broadcasted_iota(jnp.int32, (8, 128), 1)
        wave_y = (2.0 * math.pi / NY) * jnp.where(iy < NY // 2, iy, iy - NY).astype(F32)
        wave_z = (2.0 * math.pi / NZ) * jnp.where(iz < NZ // 2, iz, iz - NZ).astype(F32)
        return wave_x, wave_y, wave_z

    @pl.loop(0, WIDTH)
    def _(kx):
        wave_x, wave_y, wave_z = tile_waves(kx)
        square = wave_x * wave_x + wave_y * wave_y + wave_z * wave_z
        inverse = jnp.where(square > 0, 1.0, 0.0) / jnp.where(square > 0, square, 1.0)
        first = octet(kx)
        scale = mask_ref[first, :].astype(F32) * jnp.where(gy * WIDTH + kx == 0, 1.0, 0.5)
        for c in range(2):
            at = octet(c * WIDTH + kx)
            v0, v1, v2 = cot_ref[0, at, :], cot_ref[1, at, :], cot_ref[2, at, :]
            along = (wave_x * v0 + wave_y * v1 + wave_z * v2) * inverse
            adj[0, at, :] = scale * (v0 - wave_x * along)
            adj[1, at, :] = scale * (v1 - wave_y * along)
            adj[2, at, :] = scale * (v2 - wave_z * along)

    def z_inverse(source, f, base):
        table = (zi_ref[0], zi_ref[1])
        view = sent.reshape(10, 1024, 128)
        for pair in range(4):
            wide = []
            for ky in (2 * pair, 2 * pair + 1):
                own = source[f, pl.ds(ky, 128, stride=8), :]
                wide.append(jnp.concatenate([own, jnp.concatenate([-own[64:], own[:64]], 0)], 1))
            done = three(table, halves(jnp.concatenate(wide, 0)), dot_nt)
            for k in range(2):
                at = pl.ds(2 * pair + k, 128, stride=8)
                view[base + f, at, :] = done[:128, k * 128 : k * 128 + 128]

                @pl.when(f < 2)
                def _():
                    view[base + 3 + f, at, :] = done[128:, k * 128 : k * 128 + 128]

    def flow_first(f):
        to_rings(lambda k: sent.at[f, k], ring.at[f, :, octet(z_lo), lanes(gy)], s1.at[f], r1.at[f])

    def flow_second(f):
        drain(ring.at[f], r1.at[f])
        to_sheets(lambda k: ring.at[f, k], plane.at[f, w], s2.at[f], r2.at[f])

    def pull_first(f):
        to_sheets(lambda k: sent.at[f, :, k], sheet.at[f - 5, w], s1.at[f], r1.at[f])

    def pull_second(f):
        @pl.when(kept_x)
        def _():
            drain_tiles(88, r1.at[f])
            for first, count in ((0, 4), (4 + 5 * z_lo, 3), (12, 4)):
                some = pl.ds(first, count)
                to_rings(
                    lambda k: sheet.at[f - 5, some, k], plane.at[f + 1, some, octet(z_lo), lanes(gy)],
                    s2.at[f], r2.at[f],
                )

    @pl.loop(0, 3)
    def _(f):
        @pl.when(kept)
        def _():
            z_inverse(adj, f, 5)
            pull_first(5 + f)

            @pl.when(f < 2)
            def _():
                pull_first(8 + f)

    @pl.loop(0, 3)
    def _(f):
        z_inverse(modes_ref, f, 0)
        flow_first(f)

    @pl.loop(6, 11)
    def _(slot):
        plane[slot, :, :, 384:] = jnp.zeros((RINGS, 16, 128), F32)
        plane[slot, 4:7, 8:, :384] = jnp.zeros((3, 8, 384), F32)
        plane[slot, 7:9, :, :384] = jnp.zeros((2, 16, 384), F32)
        plane[slot, 9:12, :8, :384] = jnp.zeros((3, 8, 384), F32)

    @pl.loop(0, 3)
    def _(f):
        pull_second(5 + f)
        flow_second(f)

    @pl.loop(3, 5)
    def _(f):
        pull_second(5 + f)
        flow_first(f)

    lane = lax.broadcasted_iota(jnp.int32, (1, NX), 1)
    wave_x = (2.0 * math.pi / NX) * ((lane // 128) * WIDTH + lane % WIDTH).astype(F32)
    sign = jnp.where(lane % 128 < WIDTH, -1.0, 1.0).astype(F32)

    def turn(value):
        parts = [pltpu.roll(value[:, k * 128 : k * 128 + 128], 64, 1) for k in range(value.shape[1] // 128)]
        return jnp.concatenate(parts, 1) * sign[:, : value.shape[1]]

    def wave_y_of(block):
        row = lax.broadcasted_iota(jnp.int32, (16, 1), 0)
        mode = (block // 4) * 64 + (block % 4) * 8 + (row // 8) * 32 + row % 8
        return (2.0 * math.pi / NY) * jnp.where(mode < NY // 2, mode, mode - NY).astype(F32)

    def curl(base):
        @pl.loop(0, RINGS)
        def _(block):
            wave_y = wave_y_of(block)
            t0, t1, t2 = [turn(plane[base + k, block]) for k in range(3)]
            d0, d1 = plane[base + 3, block], plane[base + 4, block]
            plane[base + 3, block] = d0 - wave_x * t2
            plane[base + 4, block] = wave_y * t2 - d1
            plane[base + 5, block] = wave_x * t1 - wave_y * t0

    def to_cells(index):
        for h in range(2):
            cols = pl.ds(h * 256, 256)
            both = three((yi_ref[0], yi_ref[1]), halves(plane[index, :, :, cols].reshape(NY, 256)))
            rows[:, cols] = both[:NY] + turn(both[NY:])
        moved = halves(rows[...])
        for h in range(2):
            cols = pl.ds(h * 256, 256)
            done = three(moved, (xi_ref[0, :, cols], xi_ref[1, :, cols]))
            phys[index, :, cols] = done

    @pl.loop(5, 10)
    def _(f):
        drain_tiles(66, r2.at[f])

    curl(6)

    @pl.loop(0, 9)
    def _(task):
        @pl.when(task > 5)
        def _():
            drain(plane.at[task - 6], r2.at[task - 6])

        to_cells((task + 6) % 12)

    hub_x, hub_y, hub_z = turb_ref[0:1, :], turb_ref[1:2, :], turb_ref[2:3, :]
    normal_x, normal_y, thrust = turb_ref[3:4, :], turb_ref[4:5, :], turb_ref[5:6, :]
    cell_x = lax.broadcasted_iota(jnp.int32, (NX, 128), 0).astype(F32)
    hot = jnp.where(cell_x == hub_x, 1.0, 0.0).astype(BF16)
    off_y = lax.broadcasted_iota(jnp.int32, (NY, 128), 0).astype(F32) - hub_y
    off_z = (gz * 4 + gy).astype(F32) - hub_z
    disk = jnp.where(off_y * off_y + off_z * off_z <= float(RADIUS * RADIUS), 1.0, 0.0)

    def project(first, inflow):
        def column(index, mean):
            high, low = halves(phys[index] + mean)
            return dot(high, hot) + dot(low, hot)

        mixed = normal_x * column(first, inflow[0]) + normal_y * column(first + 1, inflow[1])
        return jnp.sum(disk * mixed, axis=0, keepdims=True)

    part[...] = jnp.zeros((8, 128), F32)
    part[0:1, :] = project(0, (inflow_ref[0], inflow_ref[1]))
    part[1:2, :] = project(6, (0.0, 0.0))
    to_rings(lambda k: part, part_a.at[e], sa.at[0], ra.at[0])
    flow_second(3)
    drain(visc, rv.at[0])

    @pl.loop(0, 32)
    def _(block):
        at = octet(block)
        u0, u1, u2 = [phys[k, at] + inflow_ref[k] for k in range(3)]
        p0, p1, p2 = [phys[6 + k, at] for k in range(3)]
        q1, q0, q2 = [phys[9 + k, at] for k in range(3)]
        nu = visc[at]
        phys[9, at] = p1 * u2 - p2 * u1 - nu * q0
        phys[10, at] = p2 * u0 - p0 * u2 - nu * q1
        phys[11, at] = p0 * u1 - p1 * u0 - nu * q2

    drain(part_a, ra.at[0])
    total = part_a[0]
    for k in range(1, RING):
        total = total + part_a[k]
    part_b[RINGS] = total
    to_sheets(lambda k: part_b.at[RINGS], part_b.at[w], sa.at[1], ra.at[1])

    def to_modes(source, target):
        moved = halves(phys[source])
        for h in range(2):
            cols = pl.ds(h * 256, 256)
            spectrum = three(moved, (xf_ref[0, :, cols], xf_ref[1, :, cols]))
            both = three((yf_ref[0], yf_ref[1]), halves(spectrum))
            plane[target, :, :, cols] = (both[:NY] - turn(both[NY:])).reshape(RINGS, 16, 256)

    def mine(ref, k):
        return ref.at[:, octet(k // 4), lanes(k % 4)]

    def even_first(k, slot):
        to_sheets(lambda other: plane.at[slot, other], fold.at[k // 2, w], s3.at[k], r3.at[k])

    def even_second(k):
        drain(fold.at[k // 2], r3.at[k])
        to_rings(lambda other: mine(fold.at[k // 2], other), pencil.at[k, e], s4.at[k], r4.at[k])

    def odd_first(k, slot):
        to_rings(lambda other: mine(plane.at[slot], other), turned.at[k // 2, e], s3.at[k], r3.at[k])

    def odd_second(k):
        drain(turned.at[k // 2], r3.at[k])
        to_sheets(lambda other: turned.at[k // 2, :, other], pencil.at[k, :, w], s4.at[k], r4.at[k])

    @pl.loop(0, 3)
    def _(j):
        to_modes(9 + j, 6 + j)

        @pl.when(j == 0)
        def _():
            even_first(0, 6)
            flow_second(4)

        @pl.when(j == 1)
        def _():
            odd_first(1, 7)

    drain(plane.at[3], r2.at[3])
    drain(plane.at[4], r2.at[4])
    curl(0)

    @pl.loop(3, 6)
    def _(index):
        to_cells(index)

    @pl.loop(0, 32)
    def _(block):
        at = octet(block)
        w1, w0, w2 = [phys[3 + k, at] for k in range(3)]
        p0, p1, p2 = [phys[6 + k, at] for k in range(3)]
        phys[3, at] = w1 * p2 - w2 * p1
        phys[4, at] = w2 * p0 - w0 * p2
        phys[5, at] = w0 * p1 - w1 * p0

    drain(part_b.at[pl.ds(0, RINGS)], ra.at[1])
    total = part_b[0]
    for k in range(1, RINGS):
        total = total + part_b[k]
    disk_speed = total[0:1] / disk_area()
    push = total[1:2]
    grad_ref[...] = jnp.broadcast_to(-0.5 * SECTION_STEP * disk_speed * jnp.abs(disk_speed) * push, (8, 128))
    weight = -thrust * jnp.abs(disk_speed) * push / disk_area()
    for index, normal in ((3, normal_x), (4, normal_y)):
        high, low = halves(disk * (weight * normal))
        phys[index] = phys[index] + dot_nt(high, hot) + dot_nt(low, hot)

    @pl.loop(0, 3)
    def _(j):
        to_modes(3 + j, 9 + j)

        @pl.loop(0, RINGS)
        def _(block):
            own = plane[9 + j, block]

            @pl.when(j == 0)
            def _():
                plane[9, block] = own + wave_y_of(block) * turn(plane[8, block])

            @pl.when(j == 1)
            def _():
                plane[10, block] = own - wave_x * turn(plane[8, block])

            @pl.when(j == 2)
            def _():
                plane[11, block] = own + wave_x * turn(plane[7, block]) - wave_y_of(block) * turn(plane[6, block])

        @pl.when(j == 0)
        def _():
            even_first(2, 9)
            odd_second(1)
            even_second(0)

        @pl.when(j == 1)
        def _():
            odd_first(3, 10)

        @pl.when(j == 2)
        def _():
            even_first(4, 11)

    even_second(2)
    odd_second(3)
    even_second(4)
    pencils = pencil.reshape(5, 1024, 128)

    def z_forward(f, table, fields):
        for pair in range(4):
            tall = []
            for k in fields:
                own = jnp.concatenate([pencils[k, pl.ds(2 * pair + i, 128, stride=8), :] for i in range(2)], 1)
                tall += [own, turn(own)]
            done = three(table, halves(jnp.concatenate(tall, 0)))
            for i in range(2):
                at = pl.ds(2 * pair + i, 128, stride=8)
                doubled = jnp.where(
                    (lax.broadcasted_iota(jnp.int32, (128, 1), 0) % WIDTH == 0) & (gy == 0), 1.0, 2.0
                )
                out_ref[f, at, :] = adj[f, at, :] * doubled + SECTION_STEP * done[:, i * 128 : i * 128 + 128].T

    for k in range(3):
        drain(pencil.at[k], r4.at[k])
    z_forward(0, (zf_ref[0, 0], zf_ref[1, 0]), (2, 1))
    drain(pencil.at[3], r4.at[3])
    z_forward(1, (zf_ref[0, 1], zf_ref[1, 1]), (3, 0))
    drain(pencil.at[4], r4.at[4])
    z_forward(2, (zf_ref[0, 0, :, :256], zf_ref[1, 0, :, :256]), (4,))

    @pl.loop(0, 5)
    def _(f):
        drain_tiles(112, s1.at[f])
        drain_tiles(120, s2.at[f])

        @pl.when(kept)
        def _():
            drain_tiles(120, s1.at[5 + f])

        @pl.when(kept_x)
        def _():
            drain_tiles(77, s2.at[5 + f])

        @pl.when(f % 2 == 0)
        def _():
            drain_tiles(120, s3.at[f])
            drain_tiles(112, s4.at[f])

        @pl.when(f % 2 == 1)
        def _():
            drain_tiles(112, s3.at[f])
            drain_tiles(120, s4.at[f])

    drain(visc.at[pl.ds(0, 192)], sv.at[0])
    drain(part_a.at[pl.ds(0, RING - 1)], sa.at[0])
    drain(part_b.at[pl.ds(0, RINGS - 1)], sa.at[1])


def local(velocity_hat, inflow, viscosity, cot_hat, mode_mask, hub_cells, yaw_sector, thrust):
    count = thrust.shape[0]
    angle = (yaw_sector.astype(F32) - 6.0) * (math.pi / 36.0)
    hubs = hub_cells.astype(F32)
    turbines = jnp.stack([hubs[:, 0], hubs[:, 1], hubs[:, 2], jnp.cos(angle), jnp.sin(angle), thrust, thrust, thrust])
    turbines = jnp.pad(turbines, ((0, 0), (0, 128 - count)), constant_values=-1000.0)
    vmem = pl.BlockSpec(memory_space=pltpu.VMEM)
    smem = pl.BlockSpec(memory_space=pltpu.SMEM)
    dma = pltpu.SemaphoreType.DMA
    adjoint, grad = pl.pallas_call(
        kernel,
        out_shape=(
            jax.ShapeDtypeStruct((3, 1024, 128), F32),
            jax.ShapeDtypeStruct((8, 128), F32),
        ),
        in_specs=[vmem, smem] + [vmem] * 10,
        out_specs=(vmem, vmem),
        scratch_shapes=[
            pltpu.VMEM((3, 1024, 128), F32),
            pltpu.VMEM((10, RING, RINGS, 8, 128), F32),
            pltpu.VMEM((5, RINGS, 16, NX), F32),
            pltpu.VMEM((5, RINGS, RING, 8, 128), F32),
            pltpu.VMEM((12, RINGS, 16, NX), F32),
            pltpu.VMEM((12, NY, NX), F32),
            pltpu.VMEM((NY, NX), F32),
            pltpu.VMEM((NY, NX), F32),
            pltpu.VMEM((3, RINGS, 16, NX), F32),
            pltpu.VMEM((2, RING, RINGS, 8, 128), F32),
            pltpu.VMEM((5, RING, RINGS, 8, 128), F32),
            pltpu.VMEM((8, 128), F32),
            pltpu.VMEM((RING, 8, 128), F32),
            pltpu.VMEM((RINGS + 1, 8, 128), F32),
            dma((10,)), dma((10,)), dma((10,)), dma((10,)),
            dma((5,)), dma((5,)), dma((5,)), dma((5,)),
            dma((1,)), dma((1,)), dma((2,)), dma((2,)),
        ],
        compiler_params=pltpu.CompilerParams(
            collective_id=0, has_side_effects=True, vmem_limit_bytes=60 * 1024 * 1024
        ),
    )(
        velocity_hat.reshape(3, 1024, 128),
        inflow,
        viscosity,
        cot_hat.reshape(3, 1024, 128),
        mode_mask.reshape(512, 128),
        turbines,
        *[jnp.asarray(t) for t in tables()],
    )
    return adjoint.reshape(velocity_hat.shape), grad[0, :count]


def solution(mesh):
    placed = (
        P(None, None, "gy", "gz", None),
        P(),
        P("gz", "gy", None),
        P(None, None, "gy", "gz", None),
        P("gy", "gz", None),
        P(),
        P(),
        P(),
    )
    return jax.shard_map(
        local,
        mesh=mesh,
        in_specs=placed,
        out_specs=(P(None, None, "gy", "gz", None), P()),
        check_vma=False,
    )
```

```python
import math

import jax
import jax.numpy as jnp
import ml_dtypes
import numpy as np
from jax import lax
from jax.experimental import pallas as pl
from jax.experimental.pallas import tpu as pltpu
from jax.sharding import PartitionSpec as P

MESH = pl.DeviceIdType.MESH
F32 = jnp.float32
BF16 = jnp.bfloat16
RADIUS = 4
SECTION_STEP = 0.24
NX, NY, NZ = 512, 256, 128
WIDTH = 64
RING, RINGS = 8, 16


def disk_area():
    reach = range(-RADIUS, RADIUS + 1)
    return float(sum(1 for a in reach for b in reach if a * a + b * b <= RADIUS * RADIUS))


def signed(index, length):
    return np.where(index < length // 2, index, index - length)


def split(table):
    high = table.astype(ml_dtypes.bfloat16)
    low = (table - high.astype(np.float64)).astype(ml_dtypes.bfloat16)
    return np.stack([high, low])


def tables():
    e, w = np.meshgrid(np.arange(RING), np.arange(RINGS), indexing="ij")
    cell_z = ((w // 4) * 32 + (e // 4) * 16 + (w % 4) * 4 + e % 4).reshape(-1)
    mode_z = np.arange(NZ)
    wave_z = 2.0 * math.pi / NZ * signed(mode_z, NZ)
    angle = 2.0 * math.pi / NZ * (cell_z[:, None] * mode_z[None, :] % NZ)
    cos, sin = np.cos(angle), np.sin(angle)
    z_inverse = np.block([[cos, sin], [-wave_z * sin, wave_z * cos]])
    cos, sin = cos.T, sin.T
    wave_z = wave_z[:, None]
    z_first = np.block([cos, -sin, -wave_z * sin, -wave_z * cos])
    z_second = np.block([cos, -sin, wave_z * sin, wave_z * cos])
    row = np.arange(NY)
    w, z_lo, r = row // 16, row // 8 % 2, row % 8
    mode_y = (w // 4) * 64 + z_lo * 32 + (w % 4) * 8 + r
    angle = 2.0 * math.pi / NY * (np.arange(NY)[:, None] * mode_y[None, :] % NY)
    cos, sin = np.cos(angle), np.sin(angle)
    y_inverse = np.concatenate([cos, sin])
    y_forward = np.concatenate([cos.T, sin.T])
    lane = np.arange(NX)
    mode_x = lane // 128 * WIDTH + lane % WIDTH
    weight = np.where(mode_x == 0, 1.0, 2.0) / math.sqrt(NX * NY * NZ)
    angle = 2.0 * math.pi / NX * (mode_x[:, None] * np.arange(NX)[None, :] % NX)
    real = (lane % 128 < WIDTH)[:, None]
    x_inverse = weight[:, None] * np.where(real, np.cos(angle), -np.sin(angle))
    return [split(t) for t in (z_inverse, np.stack([z_first, z_second]), y_inverse, y_forward, x_inverse, x_inverse.T)]


def halves(value):
    high = value.astype(BF16)
    return high, (value - high.astype(F32)).astype(BF16)


def dot(left, right):
    return jnp.dot(left, right, preferred_element_type=F32)


def dot_nt(left, right):
    return lax.dot_general(left, right, (((1,), (1,)), ((), ())), preferred_element_type=F32)


def three(left, right, product=dot):
    return product(left[0], right[0]) + product(left[0], right[1]) + product(left[1], right[0])


def kernel(
    inflow_ref, turb_ref, visc_ref, *refs,
):
    held, refs = refs[:9], refs[9:]
    (out_ref, grad_ref), refs = refs[:2], refs[2:]
    loaded, refs = refs[:9], refs[9:]
    cot_ref, mask_ref, zi_ref, modes_ref, yi_ref, xi_ref, xf_ref, yf_ref, zf_ref = loaded
    (
        adj, sent, ring, sheet, plane, phys, visc, rows, fold, turned, pencil, part, part_a, part_b,
        s1, r1, s2, r2, s3, r3, s4, r4, sv, rv, sa, ra, load,
    ) = refs
    gy = lax.axis_index("gy")
    gz = lax.axis_index("gz")
    x = gz // 8
    z_lo = gz // 4 % 2
    y = gz % 4
    z = gy // 2 * 2 + z_lo
    core = gy % 2
    e = z_lo * 4 + gy
    w = x * 4 + y
    kept_x = gy < 3
    kept = kept_x & ((gz < 11) | (gz > 20))

    def ring_id(other):
        return {"gy": other % 4, "gz": x * 8 + other // 4 * 4 + y}

    def sheet_id(other):
        return {"gy": gy, "gz": other // 4 * 8 + z_lo * 4 + other % 4}

    def to_ring(step):
        turn = step * 3 % RING
        there = (z + turn) % 4
        return there % 2 * 4 + there // 2 * 2 + (core + turn // 4) % 2

    def to_sheet(step):
        turn = step * 5 % RINGS
        return (x + turn // 4) % 4 * 4 + (y + turn) % 4

    barrier = pltpu.get_barrier_semaphore()

    @pl.loop(1, RING)
    def _(step):
        pl.semaphore_signal(barrier, inc=1, device_id=ring_id(to_ring(step)), device_id_type=MESH)

    @pl.loop(1, RINGS)
    def _(step):
        pl.semaphore_signal(barrier, inc=1, device_id=sheet_id(to_sheet(step)), device_id_type=MESH)

    loads = [pltpu.make_async_copy(held[k], loaded[k], load.at[k]) for k in range(9)]
    for copy in loads:
        copy.start()
    pl.semaphore_wait(barrier, RING + RINGS - 2)

    def exchange(steps, target, device, source, landing, send, receive):
        @pl.loop(1, steps)
        def _(step):
            other = target(step)
            pltpu.make_async_remote_copy(
                src_ref=source(other), dst_ref=landing, send_sem=send, recv_sem=receive,
                device_id=device(other), device_id_type=MESH,
            ).start()

        pltpu.make_async_copy(source(target(0)), landing, receive).start()

    def to_rings(source, landing, send, receive):
        exchange(RING, to_ring, ring_id, source, landing, send, receive)

    def to_sheets(source, landing, send, receive):
        exchange(RINGS, to_sheet, sheet_id, source, landing, send, receive)

    def drain(ref, sem):
        pltpu.make_async_copy(ref, ref, sem).wait()

    tiles = sent.reshape(1280, 8, 128)

    def drain_tiles(count, sem):
        drain(tiles.at[pl.ds(0, count)], sem)

    def lanes(index):
        return pl.ds(pl.multiple_of(index * 128, 128), 128)

    def octet(index):
        return pl.ds(pl.multiple_of(index * 8, 8), 8)

    landing = visc.at[pl.ds(pl.multiple_of(gy * 64, 64), 64)]

    @pl.loop(1, 4)
    def _(step):
        other = (gy + step) % 4
        pltpu.make_async_remote_copy(
            src_ref=visc_ref.at[other], dst_ref=landing, send_sem=sv.at[0], recv_sem=rv.at[0],
            device_id={"gy": other, "gz": gz}, device_id_type=MESH,
        ).start()

    pltpu.make_async_copy(visc_ref.at[gy], landing, rv.at[0]).start()

    def tile_waves(kx):
        wave_x = (2.0 * math.pi / NX) * (gy * WIDTH + kx).astype(F32)
        iy = gz * 8 + lax.broadcasted_iota(jnp.int32, (8, 128), 0)
        iz = lax.broadcasted_iota(jnp.int32, (8, 128), 1)
        wave_y = (2.0 * math.pi / NY) * jnp.where(iy < NY // 2, iy, iy - NY).astype(F32)
        wave_z = (2.0 * math.pi / NZ) * jnp.where(iz < NZ // 2, iz, iz - NZ).astype(F32)
        return wave_x, wave_y, wave_z

    loads[0].wait()
    loads[1].wait()

    @pl.loop(0, WIDTH)
    def _(kx):
        wave_x, wave_y, wave_z = tile_waves(kx)
        square = wave_x * wave_x + wave_y * wave_y + wave_z * wave_z
        inverse = jnp.where(square > 0, 1.0, 0.0) / jnp.where(square > 0, square, 1.0)
        first = octet(kx)
        scale = mask_ref[first, :].astype(F32) * jnp.where(gy * WIDTH + kx == 0, 1.0, 0.5)
        for c in range(2):
            at = octet(c * WIDTH + kx)
            v0, v1, v2 = cot_ref[0, at, :], cot_ref[1, at, :], cot_ref[2, at, :]
            along = (wave_x * v0 + wave_y * v1 + wave_z * v2) * inverse
            adj[0, at, :] = scale * (v0 - wave_x * along)
            adj[1, at, :] = scale * (v1 - wave_y * along)
            adj[2, at, :] = scale * (v2 - wave_z * along)

    def z_inverse(source, f, base):
        table = (zi_ref[0], zi_ref[1])
        view = sent.reshape(10, 1024, 128)
        for pair in range(4):
            wide = []
            for ky in (2 * pair, 2 * pair + 1):
                own = source[f, pl.ds(ky, 128, stride=8), :]
                wide.append(jnp.concatenate([own, jnp.concatenate([-own[64:], own[:64]], 0)], 1))
            done = three(table, halves(jnp.concatenate(wide, 0)), dot_nt)
            for k in range(2):
                at = pl.ds(2 * pair + k, 128, stride=8)
                view[base + f, at, :] = done[:128, k * 128 : k * 128 + 128]

                @pl.when(f < 2)
                def _():
                    view[base + 3 + f, at, :] = done[128:, k * 128 : k * 128 + 128]

    def flow_first(f):
        to_rings(lambda k: sent.at[f, k], ring.at[f, :, octet(z_lo), lanes(gy)], s1.at[f], r1.at[f])

    def flow_second(f):
        drain(ring.at[f], r1.at[f])
        to_sheets(lambda k: ring.at[f, k], plane.at[f, w], s2.at[f], r2.at[f])

    def pull_first(f):
        to_sheets(lambda k: sent.at[f, :, k], sheet.at[f - 5, w], s1.at[f], r1.at[f])

    def pull_second(f):
        @pl.when(kept_x)
        def _():
            drain_tiles(88, r1.at[f])
            for first, count in ((0, 4), (4 + 5 * z_lo, 3), (12, 4)):
                some = pl.ds(first, count)
                to_rings(
                    lambda k: sheet.at[f - 5, some, k], plane.at[f + 1, some, octet(z_lo), lanes(gy)],
                    s2.at[f], r2.at[f],
                )

    loads[2].wait()

    @pl.loop(0, 3)
    def _(f):
        @pl.when(kept)
        def _():
            z_inverse(adj, f, 5)
            pull_first(5 + f)

            @pl.when(f < 2)
            def _():
                pull_first(8 + f)

    loads[3].wait()

    @pl.loop(0, 3)
    def _(f):
        z_inverse(modes_ref, f, 0)
        flow_first(f)

    @pl.loop(6, 11)
    def _(slot):
        plane[slot, :, :, 384:] = jnp.zeros((RINGS, 16, 128), F32)
        plane[slot, 4:7, 8:, :384] = jnp.zeros((3, 8, 384), F32)
        plane[slot, 7:9, :, :384] = jnp.zeros((2, 16, 384), F32)
        plane[slot, 9:12, :8, :384] = jnp.zeros((3, 8, 384), F32)

    @pl.loop(0, 3)
    def _(f):
        pull_second(5 + f)
        flow_second(f)

    pull_second(8)
    pull_second(9)
    flow_first(3)
    flow_first(4)
    for copy in loads[4:]:
        copy.wait()

    lane = lax.broadcasted_iota(jnp.int32, (1, NX), 1)
    wave_x = (2.0 * math.pi / NX) * ((lane // 128) * WIDTH + lane % WIDTH).astype(F32)
    sign = jnp.where(lane % 128 < WIDTH, -1.0, 1.0).astype(F32)

    def turn(value):
        parts = [pltpu.roll(value[:, k * 128 : k * 128 + 128], 64, 1) for k in range(value.shape[1] // 128)]
        return jnp.concatenate(parts, 1) * sign[:, : value.shape[1]]

    def wave_y_of(block):
        row = lax.broadcasted_iota(jnp.int32, (16, 1), 0)
        mode = (block // 4) * 64 + (block % 4) * 8 + (row // 8) * 32 + row % 8
        return (2.0 * math.pi / NY) * jnp.where(mode < NY // 2, mode, mode - NY).astype(F32)

    def curl(base, slots):
        @pl.loop(0, RINGS)
        def _(block):
            wave_y = wave_y_of(block)
            if 3 in slots:
                plane[base + 3, block] = plane[base + 3, block] - wave_x * turn(plane[base + 2, block])
            if 4 in slots:
                plane[base + 4, block] = wave_y * turn(plane[base + 2, block]) - plane[base + 4, block]
            if 5 in slots:
                plane[base + 5, block] = wave_x * turn(plane[base + 1, block]) - wave_y * turn(plane[base, block])

    def to_cells(index):
        for h in range(2):
            cols = pl.ds(h * 256, 256)
            both = three((yi_ref[0], yi_ref[1]), halves(plane[index, :, :, cols].reshape(NY, 256)))
            rows[:, cols] = both[:NY] + turn(both[NY:])
        moved = halves(rows[...])
        for h in range(2):
            cols = pl.ds(h * 256, 256)
            done = three(moved, (xi_ref[0, :, cols], xi_ref[1, :, cols]))
            phys[index, :, cols] = done

    @pl.loop(0, 9)
    def _(task):
        @pl.when(task < 3)
        def _():
            drain_tiles(66, r2.at[5 + task])

        @pl.when(task == 3)
        def _():
            drain(plane.at[0], r2.at[0])

        @pl.when(task == 4)
        def _():
            drain_tiles(66, r2.at[8])
            drain_tiles(66, r2.at[9])
            curl(6, (3, 4, 5))

        @pl.when(task == 7)
        def _():
            drain(plane.at[1], r2.at[1])

        @pl.when(task == 8)
        def _():
            flow_second(3)
            drain(plane.at[2], r2.at[2])

        to_cells(jnp.where(task < 3, task + 6, jnp.where(task == 3, 0, jnp.where(task < 7, task + 5, task - 6))))

    hub_x, hub_y, hub_z = turb_ref[0:1, :], turb_ref[1:2, :], turb_ref[2:3, :]
    sector, thrust = turb_ref[3:4, :], turb_ref[4:5, :]
    normal_x = normal_y = jnp.zeros((1, 128), F32)
    for k in range(13):
        angle = (k - 6) * math.pi / 36.0
        normal_x = jnp.where(sector == float(k), math.cos(angle), normal_x)
        normal_y = jnp.where(sector == float(k), math.sin(angle), normal_y)
    cell_x = lax.broadcasted_iota(jnp.int32, (NX, 128), 0).astype(F32)
    hot = jnp.where(cell_x == hub_x, 1.0, 0.0).astype(BF16)
    off_y = lax.broadcasted_iota(jnp.int32, (NY, 128), 0).astype(F32) - hub_y
    off_z = (gz * 4 + gy).astype(F32) - hub_z
    disk = jnp.where(off_y * off_y + off_z * off_z <= float(RADIUS * RADIUS), 1.0, 0.0)

    def project(first, inflow):
        def column(index, mean):
            high, low = halves(phys[index] + mean)
            return dot(high, hot) + dot(low, hot)

        mixed = normal_x * column(first, inflow[0]) + normal_y * column(first + 1, inflow[1])
        return jnp.sum(disk * mixed, axis=0, keepdims=True)

    part[...] = jnp.zeros((8, 128), F32)
    part[0:1, :] = project(0, (inflow_ref[0], inflow_ref[1]))
    part[1:2, :] = project(6, (0.0, 0.0))
    to_rings(lambda k: part, part_a.at[e], sa.at[0], ra.at[0])
    drain(visc, rv.at[0])

    @pl.loop(0, 32)
    def _(block):
        at = octet(block)
        u0, u1, u2 = [phys[k, at] + inflow_ref[k] for k in range(3)]
        p0, p1, p2 = [phys[6 + k, at] for k in range(3)]
        q1, q0, q2 = [phys[9 + k, at] for k in range(3)]
        nu = visc[at]
        phys[9, at] = p1 * u2 - p2 * u1 - nu * q0
        phys[10, at] = p2 * u0 - p0 * u2 - nu * q1
        phys[11, at] = p0 * u1 - p1 * u0 - nu * q2

    drain(part_a, ra.at[0])
    total = part_a[0]
    for k in range(1, RING):
        total = total + part_a[k]
    part_b[RINGS] = total
    to_sheets(lambda k: part_b.at[RINGS], part_b.at[w], sa.at[1], ra.at[1])

    def to_modes(source, target):
        moved = halves(phys[source])
        for h in range(2):
            cols = pl.ds(h * 256, 256)
            spectrum = three(moved, (xf_ref[0, :, cols], xf_ref[1, :, cols]))
            both = three((yf_ref[0], yf_ref[1]), halves(spectrum))
            plane[target, :, :, cols] = (both[:NY] - turn(both[NY:])).reshape(RINGS, 16, 256)

    def mine(ref, k):
        return ref.at[:, octet(k // 4), lanes(k % 4)]

    def even_first(k, slot):
        to_sheets(lambda other: plane.at[slot, other], fold.at[k // 2, w], s3.at[k], r3.at[k])

    def even_second(k):
        drain(fold.at[k // 2], r3.at[k])
        to_rings(lambda other: mine(fold.at[k // 2], other), pencil.at[k, e], s4.at[k], r4.at[k])

    def odd_first(k, slot):
        to_rings(lambda other: mine(plane.at[slot], other), turned.at[k // 2, e], s3.at[k], r3.at[k])

    def odd_second(k):
        drain(turned.at[k // 2], r3.at[k])
        to_sheets(lambda other: turned.at[k // 2, :, other], pencil.at[k, :, w], s4.at[k], r4.at[k])

    @pl.loop(0, 3)
    def _(j):
        to_modes(9 + j, 6 + j)

        @pl.when(j == 0)
        def _():
            even_first(0, 6)
            flow_second(4)

        @pl.when(j == 1)
        def _():
            odd_first(1, 7)

    curl(0, (5,))
    to_cells(5)
    drain(plane.at[3], r2.at[3])
    curl(0, (3,))
    to_cells(3)

    @pl.loop(0, 32)
    def _(block):
        at = octet(block)
        phys[9, at] = phys[3, at] * phys[8, at] - phys[5, at] * phys[7, at]

    drain(part_b.at[pl.ds(0, RINGS)], ra.at[1])
    total = part_b[0]
    for k in range(1, RINGS):
        total = total + part_b[k]
    disk_speed = total[0:1] / disk_area()
    push = total[1:2]
    grad = -0.5 * SECTION_STEP * disk_speed * jnp.abs(disk_speed) * push
    grad_ref[...] = grad[:, : grad_ref.shape[1]]
    weight = -thrust * jnp.abs(disk_speed) * push / disk_area()

    def add_force(index, normal):
        high, low = halves(disk * (weight * normal))
        phys[index] = phys[index] + dot_nt(high, hot) + dot_nt(low, hot)

    add_force(9, normal_x)
    to_modes(9, 9)

    @pl.loop(0, RINGS)
    def _(block):
        plane[9, block] = plane[9, block] + wave_y_of(block) * turn(plane[8, block])

    even_first(2, 9)
    odd_second(1)
    drain(plane.at[4], r2.at[4])
    curl(0, (4,))
    to_cells(4)

    @pl.loop(0, 32)
    def _(block):
        at = octet(block)
        w1, w0, w2 = [phys[3 + k, at] for k in range(3)]
        p0, p1, p2 = [phys[6 + k, at] for k in range(3)]
        phys[10, at] = w2 * p0 - w0 * p2
        phys[11, at] = w0 * p1 - w1 * p0

    add_force(10, normal_y)

    @pl.loop(1, 3)
    def _(j):
        to_modes(9 + j, 9 + j)

        @pl.loop(0, RINGS)
        def _(block):
            own = plane[9 + j, block]

            @pl.when(j == 1)
            def _():
                plane[10, block] = own - wave_x * turn(plane[8, block])

            @pl.when(j == 2)
            def _():
                plane[11, block] = own + wave_x * turn(plane[7, block]) - wave_y_of(block) * turn(plane[6, block])

        @pl.when(j == 1)
        def _():
            odd_first(3, 10)
            even_second(0)

        @pl.when(j == 2)
        def _():
            even_first(4, 11)

    even_second(2)
    odd_second(3)
    even_second(4)
    pencils = pencil.reshape(5, 1024, 128)

    def z_forward(f, table, fields):
        for pair in range(4):
            tall = []
            for k in fields:
                own = jnp.concatenate([pencils[k, pl.ds(2 * pair + i, 128, stride=8), :] for i in range(2)], 1)
                tall += [own, turn(own)]
            done = three(table, halves(jnp.concatenate(tall, 0)))
            for i in range(2):
                at = pl.ds(2 * pair + i, 128, stride=8)
                doubled = jnp.where(
                    (lax.broadcasted_iota(jnp.int32, (128, 1), 0) % WIDTH == 0) & (gy == 0), 1.0, 2.0
                )
                out_ref[f, at, :] = adj[f, at, :] * doubled + SECTION_STEP * done[:, i * 128 : i * 128 + 128].T

    for k in range(3):
        drain(pencil.at[k], r4.at[k])
    z_forward(0, (zf_ref[0, 0], zf_ref[1, 0]), (2, 1))
    drain(pencil.at[3], r4.at[3])
    z_forward(1, (zf_ref[0, 1], zf_ref[1, 1]), (3, 0))
    drain(pencil.at[4], r4.at[4])
    z_forward(2, (zf_ref[0, 0, :, :256], zf_ref[1, 0, :, :256]), (4,))

    @pl.loop(0, 5)
    def _(f):
        drain_tiles(112, s1.at[f])
        drain_tiles(120, s2.at[f])

        @pl.when(kept)
        def _():
            drain_tiles(120, s1.at[5 + f])

        @pl.when(kept_x)
        def _():
            drain_tiles(77, s2.at[5 + f])

        @pl.when(f % 2 == 0)
        def _():
            drain_tiles(120, s3.at[f])
            drain_tiles(112, s4.at[f])

        @pl.when(f % 2 == 1)
        def _():
            drain_tiles(112, s3.at[f])
            drain_tiles(120, s4.at[f])

    drain(visc.at[pl.ds(0, 192)], sv.at[0])
    drain(part_a.at[pl.ds(0, RING - 1)], sa.at[0])
    drain(part_b.at[pl.ds(0, RINGS - 1)], sa.at[1])


def local(velocity_hat, inflow, viscosity, cot_hat, mode_mask, hub_cells, yaw_sector, thrust):
    count = thrust.shape[0]
    row = lax.broadcasted_iota(jnp.int32, (8, 128), 0)
    turbines = jnp.zeros((8, 128), F32)
    columns = [hub_cells[:, 0], hub_cells[:, 1], hub_cells[:, 2], yaw_sector, thrust]
    for k, column in enumerate(columns):
        padded = jnp.pad(column.astype(F32), (0, 128 - count), constant_values=-1000.0)
        turbines = jnp.where(row == k, padded[None, :], turbines)
    vmem = pl.BlockSpec(memory_space=pltpu.VMEM)
    smem = pl.BlockSpec(memory_space=pltpu.SMEM)
    dma = pltpu.SemaphoreType.DMA
    z_inverse, z_forward, y_inverse, y_forward, x_inverse, x_forward = [jnp.asarray(t) for t in tables()]
    operands = [
        cot_hat.reshape(3, 1024, 128), mode_mask.reshape(512, 128), z_inverse, velocity_hat.reshape(3, 1024, 128),
        y_inverse, x_inverse, x_forward, y_forward, z_forward,
    ]
    adjoint, grad = pl.pallas_call(
        kernel,
        out_shape=(
            jax.ShapeDtypeStruct((3, 1024, 128), F32),
            jax.ShapeDtypeStruct((1, count), F32),
        ),
        in_specs=[smem, vmem] + [pl.BlockSpec(memory_space=pl.ANY)] * 10,
        out_specs=(vmem, vmem),
        scratch_shapes=[pltpu.VMEM(each.shape, each.dtype) for each in operands] + [
            pltpu.VMEM((3, 1024, 128), F32),
            pltpu.VMEM((10, RING, RINGS, 8, 128), F32),
            pltpu.VMEM((5, RINGS, 16, NX), F32),
            pltpu.VMEM((5, RINGS, RING, 8, 128), F32),
            pltpu.VMEM((12, RINGS, 16, NX), F32),
            pltpu.VMEM((12, NY, NX), F32),
            pltpu.VMEM((NY, NX), F32),
            pltpu.VMEM((NY, NX), F32),
            pltpu.VMEM((3, RINGS, 16, NX), F32),
            pltpu.VMEM((2, RING, RINGS, 8, 128), F32),
            pltpu.VMEM((5, RING, RINGS, 8, 128), F32),
            pltpu.VMEM((8, 128), F32),
            pltpu.VMEM((RING, 8, 128), F32),
            pltpu.VMEM((RINGS + 1, 8, 128), F32),
            dma((10,)), dma((10,)), dma((10,)), dma((10,)),
            dma((5,)), dma((5,)), dma((5,)), dma((5,)),
            dma((1,)), dma((1,)), dma((2,)), dma((2,)), dma((9,)),
        ],
        compiler_params=pltpu.CompilerParams(
            collective_id=0, has_side_effects=True, vmem_limit_bytes=60 * 1024 * 1024
        ),
    )(
        inflow,
        turbines,
        viscosity,
        *operands,
    )
    return adjoint.reshape(velocity_hat.shape), grad.reshape(count)


def solution(mesh):
    placed = (
        P(None, None, "gy", "gz", None),
        P(),
        P("gz", "gy", None),
        P(None, None, "gy", "gz", None),
        P("gy", "gz", None),
        P(),
        P(),
        P(),
    )
    return jax.shard_map(
        local,
        mesh=mesh,
        in_specs=placed,
        out_specs=(P(None, None, "gy", "gz", None), P()),
        check_vma=False,
    )
```

```python
import math

import jax
import jax.numpy as jnp
import ml_dtypes
import numpy as np
from jax import lax
from jax.experimental import pallas as pl
from jax.experimental.pallas import tpu as pltpu
from jax.sharding import PartitionSpec as P

MESH = pl.DeviceIdType.MESH
F32 = jnp.float32
BF16 = jnp.bfloat16
RADIUS = 4
SECTION_STEP = 0.24
NX, NY, NZ = 512, 256, 128
WIDTH = 64
RING, RINGS = 8, 16


def disk_area():
    reach = range(-RADIUS, RADIUS + 1)
    return float(sum(1 for a in reach for b in reach if a * a + b * b <= RADIUS * RADIUS))


def signed(index, length):
    return np.where(index < length // 2, index, index - length)


def split(table):
    high = table.astype(ml_dtypes.bfloat16)
    low = (table - high.astype(np.float64)).astype(ml_dtypes.bfloat16)
    return np.stack([high, low])


def tables():
    e, w = np.meshgrid(np.arange(RING), np.arange(RINGS), indexing="ij")
    cell_z = ((w // 4) * 32 + (e // 4) * 16 + (w % 4) * 4 + e % 4).reshape(-1)
    mode_z = np.arange(NZ)
    wave_z = 2.0 * math.pi / NZ * signed(mode_z, NZ)
    angle = 2.0 * math.pi / NZ * (cell_z[:, None] * mode_z[None, :] % NZ)
    cos, sin = np.cos(angle), np.sin(angle)
    z_inverse = np.block([[cos, sin], [-wave_z * sin, wave_z * cos]])
    cos, sin = cos.T, sin.T
    wave_z = wave_z[:, None]
    z_first = np.block([cos, -sin, -wave_z * sin, -wave_z * cos])
    z_second = np.block([cos, -sin, wave_z * sin, wave_z * cos])
    row = np.arange(NY)
    w, z_lo, r = row // 16, row // 8 % 2, row % 8
    mode_y = (w // 4) * 64 + z_lo * 32 + (w % 4) * 8 + r
    angle = 2.0 * math.pi / NY * (np.arange(NY)[:, None] * mode_y[None, :] % NY)
    cos, sin = np.cos(angle), np.sin(angle)
    y_inverse = np.concatenate([cos, sin])
    y_forward = np.concatenate([cos.T, sin.T])
    lane = np.arange(NX)
    mode_x = lane // 128 * WIDTH + lane % WIDTH
    weight = np.where(mode_x == 0, 1.0, 2.0) / math.sqrt(NX * NY * NZ)
    angle = 2.0 * math.pi / NX * (mode_x[:, None] * np.arange(NX)[None, :] % NX)
    real = (lane % 128 < WIDTH)[:, None]
    x_inverse = weight[:, None] * np.where(real, np.cos(angle), -np.sin(angle))
    return [split(t) for t in (z_inverse, np.stack([z_first, z_second]), y_inverse, y_forward, x_inverse, x_inverse.T)]


def halves(value):
    high = value.astype(BF16)
    return high, (value - high.astype(F32)).astype(BF16)


def dot(left, right):
    return jnp.dot(left, right, preferred_element_type=F32)


def dot_nt(left, right):
    return lax.dot_general(left, right, (((1,), (1,)), ((), ())), preferred_element_type=F32)


def three(left, right, product=dot):
    return product(left[0], right[0]) + product(left[0], right[1]) + product(left[1], right[0])


def kernel(
    inflow_ref, hub_ref, sector_ref, thrust_ref, visc_ref, *refs,
):
    held, refs = refs[:9], refs[9:]
    (out_ref, grad_ref), refs = refs[:2], refs[2:]
    loaded, refs = refs[:9], refs[9:]
    cot_ref, mask_ref, zi_ref, modes_ref, yi_ref, xi_ref, xf_ref, yf_ref, zf_ref = loaded
    (
        adj, sent, ring, sheet, plane, phys, visc, rows, fold, turned, pencil, part, part_a, part_b, turbine,
        s1, r1, s2, r2, s3, r3, s4, r4, sv, rv, sa, ra, load,
    ) = refs
    gy = lax.axis_index("gy")
    gz = lax.axis_index("gz")
    x = gz // 8
    z_lo = gz // 4 % 2
    y = gz % 4
    z = gy // 2 * 2 + z_lo
    core = gy % 2
    e = z_lo * 4 + gy
    w = x * 4 + y
    kept_x = gy < 3
    kept = kept_x & ((gz < 11) | (gz > 20))

    def ring_id(other):
        return {"gy": other % 4, "gz": x * 8 + other // 4 * 4 + y}

    def sheet_id(other):
        return {"gy": gy, "gz": other // 4 * 8 + z_lo * 4 + other % 4}

    def to_ring(step):
        turn = step * 3 % RING
        there = (z + turn) % 4
        return there % 2 * 4 + there // 2 * 2 + (core + turn // 4) % 2

    def to_sheet(step):
        turn = step * 5 % RINGS
        return (x + turn // 4) % 4 * 4 + (y + turn) % 4

    barrier = pltpu.get_barrier_semaphore()

    @pl.loop(1, RING)
    def _(step):
        pl.semaphore_signal(barrier, inc=1, device_id=ring_id(to_ring(step)), device_id_type=MESH)

    @pl.loop(1, RINGS)
    def _(step):
        pl.semaphore_signal(barrier, inc=1, device_id=sheet_id(to_sheet(step)), device_id_type=MESH)

    loads = [pltpu.make_async_copy(held[k], loaded[k], load.at[k]) for k in range(9)]
    for copy in loads:
        copy.start()

    def exchange(steps, target, device, source, landing, send, receive):
        @pl.loop(1, steps)
        def _(step):
            other = target(step)
            pltpu.make_async_remote_copy(
                src_ref=source(other), dst_ref=landing, send_sem=send, recv_sem=receive,
                device_id=device(other), device_id_type=MESH,
            ).start()

        pltpu.make_async_copy(source(target(0)), landing, receive).start()

    def to_rings(source, landing, send, receive):
        exchange(RING, to_ring, ring_id, source, landing, send, receive)

    def to_sheets(source, landing, send, receive):
        exchange(RINGS, to_sheet, sheet_id, source, landing, send, receive)

    def drain(ref, sem):
        pltpu.make_async_copy(ref, ref, sem).wait()

    tiles = sent.reshape(1280, 8, 128)

    def drain_tiles(count, sem):
        drain(tiles.at[pl.ds(0, count)], sem)

    def lanes(index):
        return pl.ds(pl.multiple_of(index * 128, 128), 128)

    def octet(index):
        return pl.ds(pl.multiple_of(index * 8, 8), 8)

    def tile_waves(kx):
        wave_x = (2.0 * math.pi / NX) * (gy * WIDTH + kx).astype(F32)
        iy = gz * 8 + lax.broadcasted_iota(jnp.int32, (8, 128), 0)
        iz = lax.broadcasted_iota(jnp.int32, (8, 128), 1)
        wave_y = (2.0 * math.pi / NY) * jnp.where(iy < NY // 2, iy, iy - NY).astype(F32)
        wave_z = (2.0 * math.pi / NZ) * jnp.where(iz < NZ // 2, iz, iz - NZ).astype(F32)
        return wave_x, wave_y, wave_z

    loads[0].wait()
    loads[1].wait()

    @pl.loop(0, WIDTH)
    def _(kx):
        wave_x, wave_y, wave_z = tile_waves(kx)
        square = wave_x * wave_x + wave_y * wave_y + wave_z * wave_z
        inverse = jnp.where(square > 0, 1.0, 0.0) / jnp.where(square > 0, square, 1.0)
        first = octet(kx)
        scale = mask_ref[first, :].astype(F32) * jnp.where(gy * WIDTH + kx == 0, 1.0, 0.5)
        for c in range(2):
            at = octet(c * WIDTH + kx)
            v0, v1, v2 = cot_ref[0, at, :], cot_ref[1, at, :], cot_ref[2, at, :]
            along = (wave_x * v0 + wave_y * v1 + wave_z * v2) * inverse
            adj[0, at, :] = scale * (v0 - wave_x * along)
            adj[1, at, :] = scale * (v1 - wave_y * along)
            adj[2, at, :] = scale * (v2 - wave_z * along)

    def z_inverse(source, f, base):
        table = (zi_ref[0], zi_ref[1])
        view = sent.reshape(10, 1024, 128)
        for pair in range(4):
            wide = []
            for ky in (2 * pair, 2 * pair + 1):
                own = source[f, pl.ds(ky, 128, stride=8), :]
                wide.append(jnp.concatenate([own, jnp.concatenate([-own[64:], own[:64]], 0)], 1))
            done = three(table, halves(jnp.concatenate(wide, 0)), dot_nt)
            for k in range(2):
                at = pl.ds(2 * pair + k, 128, stride=8)
                view[base + f, at, :] = done[:128, k * 128 : k * 128 + 128]

                @pl.when(f < 2)
                def _():
                    view[base + 3 + f, at, :] = done[128:, k * 128 : k * 128 + 128]

    def flow_first(f):
        to_rings(lambda k: sent.at[f, k], ring.at[f, :, octet(z_lo), lanes(gy)], s1.at[f], r1.at[f])

    def flow_second(f):
        drain(ring.at[f], r1.at[f])
        to_sheets(lambda k: ring.at[f, k], plane.at[f, w], s2.at[f], r2.at[f])

    def pull_first(f):
        to_sheets(lambda k: sent.at[f, :, k], sheet.at[f - 4, w], s1.at[f], r1.at[f])

    def last_second():
        drain(sheet.at[0], r1.at[4])
        to_rings(lambda k: sheet.at[0, :, k], plane.at[4, :, octet(z_lo), lanes(gy)], s2.at[4], r2.at[4])

    def pull_second(f):
        @pl.when(kept_x)
        def _():
            drain_tiles(88, r1.at[f])
            for first, count in ((0, 4), (4 + 5 * z_lo, 3), (12, 4)):
                some = pl.ds(first, count)
                to_rings(
                    lambda k: sheet.at[f - 4, some, k], plane.at[f + 1, some, octet(z_lo), lanes(gy)],
                    s2.at[f], r2.at[f],
                )

    def send_visc():
        landing = visc.at[pl.ds(pl.multiple_of(gy * 64, 64), 64)]

        @pl.loop(1, 4)
        def _(step):
            other = (gy + step) % 4
            pltpu.make_async_remote_copy(
                src_ref=visc_ref.at[other], dst_ref=landing, send_sem=sv.at[0], recv_sem=rv.at[0],
                device_id={"gy": other, "gz": gz}, device_id_type=MESH,
            ).start()

        pltpu.make_async_copy(visc_ref.at[gy], landing, rv.at[0]).start()

    def pull_fields(f):
        pull_first(5 + f)

        @pl.when(f < 2)
        def _():
            pull_first(8 + f)

    loads[2].wait()

    @pl.when(kept)
    def _():
        z_inverse(adj, 0, 5)

    loads[3].wait()
    z_inverse(modes_ref, 0, 0)
    pl.semaphore_wait(barrier, RING + RINGS - 2)

    @pl.when(kept)
    def _():
        pull_fields(0)

    flow_first(0)
    @pl.loop(1, 3)
    def _(f):
        @pl.when(kept)
        def _():
            z_inverse(adj, f, 5)
            pull_fields(f)

        z_inverse(modes_ref, f, 0)

        @pl.when(f == 1)
        def _():
            flow_first(1)

    @pl.loop(6, 11)
    def _(slot):
        plane[slot, :, :, 384:] = jnp.zeros((RINGS, 16, 128), F32)
        plane[slot, 4:7, 8:, :384] = jnp.zeros((3, 8, 384), F32)
        plane[slot, 7:9, :, :384] = jnp.zeros((2, 16, 384), F32)
        plane[slot, 9:12, :8, :384] = jnp.zeros((3, 8, 384), F32)

    pull_second(5)
    pull_second(8)
    flow_second(0)
    pull_second(6)
    flow_first(2)
    for copy in loads[4:]:
        copy.wait()

    lane = lax.broadcasted_iota(jnp.int32, (1, NX), 1)
    wave_x = (2.0 * math.pi / NX) * ((lane // 128) * WIDTH + lane % WIDTH).astype(F32)
    sign = jnp.where(lane % 128 < WIDTH, -1.0, 1.0).astype(F32)

    def turn(value):
        parts = [pltpu.roll(value[:, k * 128 : k * 128 + 128], 64, 1) for k in range(value.shape[1] // 128)]
        return jnp.concatenate(parts, 1) * sign[:, : value.shape[1]]

    def wave_y_of(block):
        row = lax.broadcasted_iota(jnp.int32, (16, 1), 0)
        mode = (block // 4) * 64 + (block % 4) * 8 + (row // 8) * 32 + row % 8
        return (2.0 * math.pi / NY) * jnp.where(mode < NY // 2, mode, mode - NY).astype(F32)

    def curl(base, slots):
        @pl.loop(0, RINGS)
        def _(block):
            wave_y = wave_y_of(block)
            if 3 in slots:
                plane[base + 3, block] = plane[base + 3, block] - wave_x * turn(plane[base + 2, block])
            if 4 in slots:
                plane[base + 4, block] = wave_y * turn(plane[base + 2, block]) - plane[base + 4, block]
            if 5 in slots:
                plane[base + 5, block] = wave_x * turn(plane[base + 1, block]) - wave_y * turn(plane[base, block])

    def to_cells(index):
        for h in range(2):
            cols = pl.ds(h * 256, 256)
            both = three((yi_ref[0], yi_ref[1]), halves(plane[index, :, :, cols].reshape(NY, 256)))
            rows[:, cols] = both[:NY] + turn(both[NY:])
        moved = halves(rows[...])
        for h in range(2):
            cols = pl.ds(h * 256, 256)
            done = three(moved, (xi_ref[0, :, cols], xi_ref[1, :, cols]))
            phys[index, :, cols] = done

    count = thrust_ref.shape[1]
    turbine[...] = jnp.full((8, 128), -1000.0, F32)
    turbine[0:3, :count] = hub_ref[...].astype(F32)
    turbine[3:4, :count] = sector_ref[...].astype(F32)
    turbine[4:5, :count] = thrust_ref[...]
    hub_x, hub_y, hub_z, sector, thrust = [turbine[k : k + 1, :] for k in range(5)]
    normal_x = normal_y = jnp.zeros((1, 128), F32)
    for k in range(13):
        angle = (k - 6) * math.pi / 36.0
        normal_x = jnp.where(sector == float(k), math.cos(angle), normal_x)
        normal_y = jnp.where(sector == float(k), math.sin(angle), normal_y)
    cell_x = lax.broadcasted_iota(jnp.int32, (NX, 128), 0).astype(F32)
    hot = jnp.where(cell_x == hub_x, 1.0, 0.0).astype(BF16)
    off_y = lax.broadcasted_iota(jnp.int32, (NY, 128), 0).astype(F32) - hub_y
    off_z = (gz * 4 + gy).astype(F32) - hub_z
    disk = jnp.where(off_y * off_y + off_z * off_z <= float(RADIUS * RADIUS), 1.0, 0.0)

    def project(first, inflow):
        def column(index, mean):
            high, low = halves(phys[index] + mean)
            return dot(high, hot) + dot(low, hot)

        mixed = normal_x * column(first, inflow[0]) + normal_y * column(first + 1, inflow[1])
        return jnp.sum(disk * mixed, axis=0, keepdims=True)

    @pl.loop(0, 9)
    def _(task):
        @pl.when(task == 0)
        def _():
            drain_tiles(66, r2.at[5])

        @pl.when(task == 1)
        def _():
            flow_second(1)
            pull_second(9)
            drain_tiles(66, r2.at[6])

        @pl.when(task == 2)
        def _():
            pull_second(7)
            send_visc()
            flow_first(3)
            flow_second(2)
            pull_first(4)
            drain(plane.at[0], r2.at[0])

        @pl.when(task == 3)
        def _():
            for f in (7, 8, 9):
                drain_tiles(66, r2.at[f])
            curl(6, (3, 4, 5))

        @pl.when(task == 7)
        def _():
            drain(plane.at[1], r2.at[1])

        @pl.when(task == 8)
        def _():
            part[...] = jnp.zeros((8, 128), F32)
            part[0:1, :] = project(0, (inflow_ref[0], inflow_ref[1]))
            part[1:2, :] = project(6, (0.0, 0.0))
            to_rings(lambda k: part, part_a.at[e], sa.at[0], ra.at[0])
            drain(plane.at[2], r2.at[2])

        to_cells(jnp.where(task < 2, task + 6, jnp.where(task == 2, 0, jnp.where(task < 7, task + 5, task - 6))))

    drain(visc, rv.at[0])

    @pl.loop(0, 32)
    def _(block):
        at = octet(block)
        u0, u1, u2 = [phys[k, at] + inflow_ref[k] for k in range(3)]
        p0, p1, p2 = [phys[6 + k, at] for k in range(3)]
        q1, q0, q2 = [phys[9 + k, at] for k in range(3)]
        nu = visc[at]
        phys[9, at] = p1 * u2 - p2 * u1 - nu * q0
        phys[10, at] = p2 * u0 - p0 * u2 - nu * q1
        phys[11, at] = p0 * u1 - p1 * u0 - nu * q2

    flow_second(3)

    def to_modes(source, target):
        moved = halves(phys[source])
        for h in range(2):
            cols = pl.ds(h * 256, 256)
            spectrum = three(moved, (xf_ref[0, :, cols], xf_ref[1, :, cols]))
            both = three((yf_ref[0], yf_ref[1]), halves(spectrum))
            plane[target, :, :, cols] = (both[:NY] - turn(both[NY:])).reshape(RINGS, 16, 256)

    def mine(ref, k):
        return ref.at[:, octet(k // 4), lanes(k % 4)]

    def sheet_first(k, slot, at):
        to_sheets(lambda other: plane.at[slot, other], fold.at[at, w], s3.at[k], r3.at[k])

    def sheet_second(k, at):
        drain(fold.at[at], r3.at[k])
        to_rings(lambda other: mine(fold.at[at], other), pencil.at[k, e], s4.at[k], r4.at[k])

    def ring_first(k, slot, at):
        to_rings(lambda other: mine(plane.at[slot], other), turned.at[at, e], s3.at[k], r3.at[k])

    def ring_second(k, at):
        drain(turned.at[at], r3.at[k])
        to_sheets(lambda other: turned.at[at, :, other], pencil.at[k, :, w], s4.at[k], r4.at[k])

    @pl.loop(0, 3)
    def _(j):
        to_modes(9 + j, 6 + j)

        @pl.when(j == 0)
        def _():
            ring_first(0, 6, 0)
            drain(part_a, ra.at[0])
            total = part_a[0]
            for k in range(1, RING):
                total = total + part_a[k]
            part_b[RINGS] = total
            to_sheets(lambda k: part_b.at[RINGS], part_b.at[w], sa.at[1], ra.at[1])
            last_second()

        @pl.when(j == 1)
        def _():
            sheet_first(1, 7, 0)

    curl(0, (5,))
    to_cells(5)
    drain(part_b.at[pl.ds(0, RINGS)], ra.at[1])
    total = part_b[0]
    for k in range(1, RINGS):
        total = total + part_b[k]
    disk_speed = total[0:1] / disk_area()
    push = total[1:2]
    grad = -0.5 * SECTION_STEP * disk_speed * jnp.abs(disk_speed) * push
    grad_ref[...] = grad[:, : grad_ref.shape[1]]
    weight = -thrust * jnp.abs(disk_speed) * push / disk_area()

    for index, normal in ((9, normal_x), (10, normal_y)):
        high, low = halves(disk * (weight * normal))
        phys[index] = dot_nt(high, hot) + dot_nt(low, hot)

    drain(plane.at[3], r2.at[3])
    curl(0, (3,))
    to_cells(3)

    @pl.loop(0, 32)
    def _(block):
        at = octet(block)
        phys[9, at] = phys[9, at] + phys[3, at] * phys[8, at] - phys[5, at] * phys[7, at]

    to_modes(9, 9)

    @pl.loop(0, RINGS)
    def _(block):
        plane[9, block] = plane[9, block] + wave_y_of(block) * turn(plane[8, block])

    ring_first(2, 9, 1)
    ring_second(0, 0)
    drain(plane.at[4], r2.at[4])
    curl(0, (4,))
    to_cells(4)

    @pl.loop(0, 32)
    def _(block):
        at = octet(block)
        w1, w0, w2 = [phys[3 + k, at] for k in range(3)]
        p0, p1, p2 = [phys[6 + k, at] for k in range(3)]
        phys[10, at] = phys[10, at] + w2 * p0 - w0 * p2
        phys[11, at] = w0 * p1 - w1 * p0

    @pl.loop(1, 3)
    def _(j):
        to_modes(9 + j, 9 + j)

        @pl.loop(0, RINGS)
        def _(block):
            own = plane[9 + j, block]

            @pl.when(j == 1)
            def _():
                plane[10, block] = own - wave_x * turn(plane[8, block])

            @pl.when(j == 2)
            def _():
                plane[11, block] = own + wave_x * turn(plane[7, block]) - wave_y_of(block) * turn(plane[6, block])

        @pl.when(j == 1)
        def _():
            sheet_first(3, 10, 1)
            sheet_second(1, 0)

        @pl.when(j == 2)
        def _():
            sheet_first(4, 11, 2)

    ring_second(2, 1)
    sheet_second(3, 1)
    sheet_second(4, 2)
    pencils = pencil.reshape(5, 1024, 128)

    def z_forward(f, table, fields):
        for pair in range(4):
            tall = []
            for k in fields:
                own = jnp.concatenate([pencils[k, pl.ds(2 * pair + i, 128, stride=8), :] for i in range(2)], 1)
                tall += [own, turn(own)]
            done = three(table, halves(jnp.concatenate(tall, 0)))
            for i in range(2):
                at = pl.ds(2 * pair + i, 128, stride=8)
                doubled = jnp.where(
                    (lax.broadcasted_iota(jnp.int32, (128, 1), 0) % WIDTH == 0) & (gy == 0), 1.0, 2.0
                )
                out_ref[f, at, :] = adj[f, at, :] * doubled + SECTION_STEP * done[:, i * 128 : i * 128 + 128].T

    for k in range(3):
        drain(pencil.at[k], r4.at[k])
    z_forward(0, (zf_ref[0, 0], zf_ref[1, 0]), (2, 1))
    drain(pencil.at[3], r4.at[3])
    z_forward(1, (zf_ref[0, 1], zf_ref[1, 1]), (3, 0))
    drain(pencil.at[4], r4.at[4])
    z_forward(2, (zf_ref[0, 0, :, :256], zf_ref[1, 0, :, :256]), (4,))

    for f in range(4):
        drain_tiles(112, s1.at[f])
        drain_tiles(120, s2.at[f])
    drain_tiles(120, s1.at[4])
    drain_tiles(112, s2.at[4])
    for k in range(5):
        drain_tiles(112 if k in (0, 2) else 120, s3.at[k])
        drain_tiles(120 if k in (0, 2) else 112, s4.at[k])

    @pl.when(kept)
    def _():
        for f in range(5, 10):
            drain_tiles(120, s1.at[f])

    @pl.when(kept_x)
    def _():
        for f in range(5, 10):
            drain_tiles(77, s2.at[f])

    drain(visc.at[pl.ds(0, 192)], sv.at[0])
    drain(part_a.at[pl.ds(0, RING - 1)], sa.at[0])
    drain(part_b.at[pl.ds(0, RINGS - 1)], sa.at[1])


def local(velocity_hat, inflow, viscosity, cot_hat, mode_mask, hub_cells, yaw_sector, thrust):
    count = thrust.shape[0]
    vmem = pl.BlockSpec(memory_space=pltpu.VMEM)
    smem = pl.BlockSpec(memory_space=pltpu.SMEM)
    dma = pltpu.SemaphoreType.DMA
    z_inverse, z_forward, y_inverse, y_forward, x_inverse, x_forward = [jnp.asarray(t) for t in tables()]
    operands = [
        cot_hat.reshape(3, 1024, 128), mode_mask.reshape(512, 128), z_inverse, velocity_hat.reshape(3, 1024, 128),
        y_inverse, x_inverse, x_forward, y_forward, z_forward,
    ]
    adjoint, grad = pl.pallas_call(
        kernel,
        out_shape=(
            jax.ShapeDtypeStruct((3, 1024, 128), F32),
            jax.ShapeDtypeStruct((1, count), F32),
        ),
        in_specs=[smem, vmem, vmem, vmem] + [pl.BlockSpec(memory_space=pl.ANY)] * 10,
        out_specs=(vmem, vmem),
        scratch_shapes=[pltpu.VMEM(each.shape, each.dtype) for each in operands] + [
            pltpu.VMEM((3, 1024, 128), F32),
            pltpu.VMEM((10, RING, RINGS, 8, 128), F32),
            pltpu.VMEM((4, RINGS, 16, NX), F32),
            pltpu.VMEM((6, RINGS, RING, 8, 128), F32),
            pltpu.VMEM((12, RINGS, 16, NX), F32),
            pltpu.VMEM((12, NY, NX), F32),
            pltpu.VMEM((NY, NX), F32),
            pltpu.VMEM((NY, NX), F32),
            pltpu.VMEM((3, RINGS, 16, NX), F32),
            pltpu.VMEM((2, RING, RINGS, 8, 128), F32),
            pltpu.VMEM((5, RING, RINGS, 8, 128), F32),
            pltpu.VMEM((8, 128), F32),
            pltpu.VMEM((RING, 8, 128), F32),
            pltpu.VMEM((RINGS + 1, 8, 128), F32),
            pltpu.VMEM((8, 128), F32),
            dma((10,)), dma((10,)), dma((10,)), dma((10,)),
            dma((5,)), dma((5,)), dma((5,)), dma((5,)),
            dma((1,)), dma((1,)), dma((2,)), dma((2,)), dma((9,)),
        ],
        compiler_params=pltpu.CompilerParams(
            collective_id=0, has_side_effects=True, vmem_limit_bytes=60 * 1024 * 1024
        ),
    )(
        inflow,
        hub_cells.T,
        yaw_sector.reshape(1, count),
        thrust.reshape(1, count),
        viscosity,
        *operands,
    )
    return adjoint.reshape(velocity_hat.shape), grad.reshape(count)


def solution(mesh):
    placed = (
        P(None, None, "gy", "gz", None),
        P(),
        P("gz", "gy", None),
        P(None, None, "gy", "gz", None),
        P("gy", "gz", None),
        P(),
        P(),
        P(),
    )
    return jax.shard_map(
        local,
        mesh=mesh,
        in_specs=placed,
        out_specs=(P(None, None, "gy", "gz", None), P()),
        check_vma=False,
    )
```

```python
import math

import jax
import jax.numpy as jnp
import ml_dtypes
import numpy as np
from jax import lax
from jax.experimental import pallas as pl
from jax.experimental.pallas import tpu as pltpu
from jax.sharding import PartitionSpec as P

MESH = pl.DeviceIdType.MESH
F32 = jnp.float32
BF16 = jnp.bfloat16
RADIUS = 4
SECTION_STEP = 0.24
NX, NY, NZ = 512, 256, 128
WIDTH = 64
RING, RINGS = 8, 16


def disk_area():
    reach = range(-RADIUS, RADIUS + 1)
    return float(sum(1 for a in reach for b in reach if a * a + b * b <= RADIUS * RADIUS))


def signed(index, length):
    return np.where(index < length // 2, index, index - length)


def split(table):
    high = table.astype(ml_dtypes.bfloat16)
    low = (table - high.astype(np.float64)).astype(ml_dtypes.bfloat16)
    return np.stack([high, low])


def tables():
    e, w = np.meshgrid(np.arange(RING), np.arange(RINGS), indexing="ij")
    cell_z = ((w // 4) * 32 + (e // 4) * 16 + (w % 4) * 4 + e % 4).reshape(-1)
    mode_z = np.arange(NZ)
    wave_z = 2.0 * math.pi / NZ * signed(mode_z, NZ)
    angle = 2.0 * math.pi / NZ * (cell_z[:, None] * mode_z[None, :] % NZ)
    cos, sin = np.cos(angle), np.sin(angle)
    z_inverse = np.block([[cos, sin], [-wave_z * sin, wave_z * cos]])
    cos, sin = cos.T, sin.T
    wave_z = wave_z[:, None]
    z_first = np.block([cos, -sin, -wave_z * sin, -wave_z * cos])
    z_second = np.block([cos, -sin, wave_z * sin, wave_z * cos])
    row = np.arange(NY)
    w, z_lo, r = row // 16, row // 8 % 2, row % 8
    mode_y = (w // 4) * 64 + z_lo * 32 + (w % 4) * 8 + r
    angle = 2.0 * math.pi / NY * (np.arange(NY // 2 + 1)[:, None] * mode_y[None, :] % NY)
    cos, sin = np.cos(angle), np.sin(angle)
    y_inverse = np.concatenate([cos, sin[1 : NY // 2]])
    lane = np.arange(NX)
    mode_x = lane // 128 * WIDTH + lane % WIDTH
    weight = np.where(mode_x == 0, 1.0, 2.0) / math.sqrt(NX * NY * NZ)
    angle = 2.0 * math.pi / NX * (mode_x[:, None] * np.arange(NX)[None, :] % NX)
    real = (lane % 128 < WIDTH)[:, None]
    x_inverse = weight[:, None] * np.where(real, np.cos(angle), -np.sin(angle))
    return [split(t) for t in (z_inverse, np.stack([z_first, z_second]), y_inverse, y_inverse.T, x_inverse, x_inverse.T)]


def halves(value):
    high = value.astype(BF16)
    return high, (value - high.astype(F32)).astype(BF16)


def dot(left, right):
    return jnp.dot(left, right, preferred_element_type=F32)


def dot_nt(left, right):
    return lax.dot_general(left, right, (((1,), (1,)), ((), ())), preferred_element_type=F32)


def three(left, right, product=dot):
    return product(left[0], right[0]) + product(left[0], right[1]) + product(left[1], right[0])


def kernel(
    inflow_ref, hub_ref, sector_ref, thrust_ref, visc_ref, *refs,
):
    held, refs = refs[:9], refs[9:]
    (out_ref, grad_ref), refs = refs[:2], refs[2:]
    loaded, refs = refs[:9], refs[9:]
    cot_ref, mask_ref, zi_ref, modes_ref, yi_ref, xi_ref, xf_ref, yf_ref, zf_ref = loaded
    (
        adj, sent, ring, sheet, plane, phys, visc, rows, fold, turned, pencil, part, part_a, part_b, turbine,
        s1, r1, s2, r2, s3, r3, s4, r4, sv, rv, sa, ra, load,
    ) = refs
    gy = lax.axis_index("gy")
    gz = lax.axis_index("gz")
    x = gz // 8
    z_lo = gz // 4 % 2
    y = gz % 4
    z = gy // 2 * 2 + z_lo
    core = gy % 2
    e = z_lo * 4 + gy
    w = x * 4 + y
    kept_x = gy < 3
    kept = kept_x & ((gz < 11) | (gz > 20))

    def ring_id(other):
        return {"gy": other % 4, "gz": x * 8 + other // 4 * 4 + y}

    def sheet_id(other):
        return {"gy": gy, "gz": other // 4 * 8 + z_lo * 4 + other % 4}

    def to_ring(step):
        turn = step * 3 % RING
        there = (z + turn) % 4
        return there % 2 * 4 + there // 2 * 2 + (core + turn // 4) % 2

    def to_sheet(step):
        turn = step * 5 % RINGS
        return (x + turn // 4) % 4 * 4 + (y + turn) % 4

    barrier = pltpu.get_barrier_semaphore()

    @pl.loop(1, RING)
    def _(step):
        pl.semaphore_signal(barrier, inc=1, device_id=ring_id(to_ring(step)), device_id_type=MESH)

    @pl.loop(1, RINGS)
    def _(step):
        pl.semaphore_signal(barrier, inc=1, device_id=sheet_id(to_sheet(step)), device_id_type=MESH)

    loads = [pltpu.make_async_copy(held[k], loaded[k], load.at[k]) for k in range(9)]
    for copy in loads:
        copy.start()

    def exchange(steps, target, device, source, landing, send, receive):
        @pl.loop(1, steps)
        def _(step):
            other = target(step)
            pltpu.make_async_remote_copy(
                src_ref=source(other), dst_ref=landing, send_sem=send, recv_sem=receive,
                device_id=device(other), device_id_type=MESH,
            ).start()

        pltpu.make_async_copy(source(target(0)), landing, receive).start()

    def to_rings(source, landing, send, receive):
        exchange(RING, to_ring, ring_id, source, landing, send, receive)

    def to_sheets(source, landing, send, receive):
        exchange(RINGS, to_sheet, sheet_id, source, landing, send, receive)

    def drain(ref, sem):
        pltpu.make_async_copy(ref, ref, sem).wait()

    tiles = sent.reshape(1280, 8, 128)

    def drain_tiles(count, sem):
        drain(tiles.at[pl.ds(0, count)], sem)

    def lanes(index):
        return pl.ds(pl.multiple_of(index * 128, 128), 128)

    def octet(index):
        return pl.ds(pl.multiple_of(index * 8, 8), 8)

    def tile_waves(kx):
        wave_x = (2.0 * math.pi / NX) * (gy * WIDTH + kx).astype(F32)
        iy = gz * 8 + lax.broadcasted_iota(jnp.int32, (8, 128), 0)
        iz = lax.broadcasted_iota(jnp.int32, (8, 128), 1)
        wave_y = (2.0 * math.pi / NY) * jnp.where(iy < NY // 2, iy, iy - NY).astype(F32)
        wave_z = (2.0 * math.pi / NZ) * jnp.where(iz < NZ // 2, iz, iz - NZ).astype(F32)
        return wave_x, wave_y, wave_z

    loads[0].wait()
    loads[1].wait()

    @pl.loop(0, WIDTH)
    def _(kx):
        wave_x, wave_y, wave_z = tile_waves(kx)
        square = wave_x * wave_x + wave_y * wave_y + wave_z * wave_z
        inverse = jnp.where(square > 0, 1.0, 0.0) / jnp.where(square > 0, square, 1.0)
        first = octet(kx)
        scale = mask_ref[first, :].astype(F32) * jnp.where(gy * WIDTH + kx == 0, 1.0, 0.5)
        for c in range(2):
            at = octet(c * WIDTH + kx)
            v0, v1, v2 = cot_ref[0, at, :], cot_ref[1, at, :], cot_ref[2, at, :]
            along = (wave_x * v0 + wave_y * v1 + wave_z * v2) * inverse
            adj[0, at, :] = scale * (v0 - wave_x * along)
            adj[1, at, :] = scale * (v1 - wave_y * along)
            adj[2, at, :] = scale * (v2 - wave_z * along)

    def z_inverse(source, f, base):
        table = (zi_ref[0], zi_ref[1])
        view = sent.reshape(10, 1024, 128)
        for pair in range(4):
            wide = []
            for ky in (2 * pair, 2 * pair + 1):
                own = source[f, pl.ds(ky, 128, stride=8), :]
                wide.append(jnp.concatenate([own, jnp.concatenate([-own[64:], own[:64]], 0)], 1))
            done = three(table, halves(jnp.concatenate(wide, 0)), dot_nt)
            for k in range(2):
                at = pl.ds(2 * pair + k, 128, stride=8)
                view[base + f, at, :] = done[:128, k * 128 : k * 128 + 128]

                @pl.when(f < 2)
                def _():
                    view[base + 3 + f, at, :] = done[128:, k * 128 : k * 128 + 128]

    def flow_first(f):
        to_rings(lambda k: sent.at[f, k], ring.at[f, :, octet(z_lo), lanes(gy)], s1.at[f], r1.at[f])

    def flow_second(f):
        drain(ring.at[f], r1.at[f])
        to_sheets(lambda k: ring.at[f, k], plane.at[f, w], s2.at[f], r2.at[f])

    def pull_first(f):
        to_sheets(lambda k: sent.at[f, :, k], sheet.at[f - 4, w], s1.at[f], r1.at[f])

    def last_second():
        drain(sheet.at[0], r1.at[4])
        to_rings(lambda k: sheet.at[0, :, k], plane.at[4, :, octet(z_lo), lanes(gy)], s2.at[4], r2.at[4])

    def pull_second(f):
        @pl.when(kept_x)
        def _():
            drain_tiles(88, r1.at[f])
            for first, count in ((0, 4), (4 + 5 * z_lo, 3), (12, 4)):
                some = pl.ds(first, count)
                to_rings(
                    lambda k: sheet.at[f - 4, some, k], plane.at[f + 1, some, octet(z_lo), lanes(gy)],
                    s2.at[f], r2.at[f],
                )

    def send_visc():
        landing = visc.at[pl.ds(pl.multiple_of(gy * 64, 64), 64)]

        @pl.loop(1, 4)
        def _(step):
            other = (gy + step) % 4
            pltpu.make_async_remote_copy(
                src_ref=visc_ref.at[other], dst_ref=landing, send_sem=sv.at[0], recv_sem=rv.at[0],
                device_id={"gy": other, "gz": gz}, device_id_type=MESH,
            ).start()

        pltpu.make_async_copy(visc_ref.at[gy], landing, rv.at[0]).start()

    def pull_fields(f):
        pull_first(5 + f)

        @pl.when(f == 0)
        def _():
            pull_first(8)

        @pl.when(f == 2)
        def _():
            pull_first(9)

    loads[2].wait()

    @pl.when(kept)
    def _():
        z_inverse(adj, 0, 5)

    loads[3].wait()
    z_inverse(modes_ref, 0, 0)
    pl.semaphore_wait(barrier, RING + RINGS - 2)

    @pl.when(kept)
    def _():
        pull_fields(0)

    flow_first(0)
    @pl.loop(1, 3)
    def _(f):
        @pl.when(kept)
        def _():
            z_inverse(adj, f, 5)
            pull_fields(f)

        z_inverse(modes_ref, f, 0)

        @pl.when(f == 1)
        def _():
            flow_first(1)

    @pl.loop(6, 11)
    def _(slot):
        plane[slot, :, :, 384:] = jnp.zeros((RINGS, 16, 128), F32)
        plane[slot, 4:7, 8:, :384] = jnp.zeros((3, 8, 384), F32)
        plane[slot, 7:9, :, :384] = jnp.zeros((2, 16, 384), F32)
        plane[slot, 9:12, :8, :384] = jnp.zeros((3, 8, 384), F32)

    pull_second(5)
    pull_second(8)
    flow_second(0)
    pull_second(6)
    flow_first(2)
    for copy in loads[4:]:
        copy.wait()

    lane = lax.broadcasted_iota(jnp.int32, (1, NX), 1)
    wave_x = (2.0 * math.pi / NX) * ((lane // 128) * WIDTH + lane % WIDTH).astype(F32)
    sign = jnp.where(lane % 128 < WIDTH, -1.0, 1.0).astype(F32)

    def turn(value):
        parts = [pltpu.roll(value[:, k * 128 : k * 128 + 128], 64, 1) for k in range(value.shape[1] // 128)]
        return jnp.concatenate(parts, 1) * sign[:, : value.shape[1]]

    def wave_y_of(block):
        row = lax.broadcasted_iota(jnp.int32, (16, 1), 0)
        mode = (block // 4) * 64 + (block % 4) * 8 + (row // 8) * 32 + row % 8
        return (2.0 * math.pi / NY) * jnp.where(mode < NY // 2, mode, mode - NY).astype(F32)

    def curl(base, slots):
        @pl.loop(0, RINGS)
        def _(block):
            wave_y = wave_y_of(block)
            if 3 in slots:
                plane[base + 3, block] = plane[base + 3, block] - wave_x * turn(plane[base + 2, block])
            if 4 in slots:
                plane[base + 4, block] = wave_y * turn(plane[base + 2, block]) - plane[base + 4, block]
            if 5 in slots:
                plane[base + 5, block] = wave_x * turn(plane[base + 1, block]) - wave_y * turn(plane[base, block])

    half = NY // 2
    edge = lax.broadcasted_iota(jnp.int32, (half, 256), 0) == 0

    def to_cells(index):
        for h in range(2):
            cols = pl.ds(h * 256, 256)
            both = three((yi_ref[0], yi_ref[1]), halves(plane[index, :, :, cols].reshape(NY, 256)))
            top, low = both[:half], both[half:]
            spun = turn(low)
            rows[:half, cols] = jnp.where(edge, top, top + spun)
            rows[half:, cols] = jnp.where(edge, low, top - spun)
        moved = halves(rows[...])
        for h in range(2):
            cols = pl.ds(h * 256, 256)
            done = three(moved, (xi_ref[0, :, cols], xi_ref[1, :, cols]))
            phys[index, :, cols] = done

    count = thrust_ref.shape[1]
    turbine[...] = jnp.full((8, 128), -1000.0, F32)
    turbine[0:3, :count] = hub_ref[...].astype(F32)
    turbine[3:4, :count] = sector_ref[...].astype(F32)
    turbine[4:5, :count] = thrust_ref[...]
    hub_x, hub_y, hub_z, sector, thrust = [turbine[k : k + 1, :] for k in range(5)]
    normal_x = normal_y = jnp.zeros((1, 128), F32)
    for k in range(13):
        angle = (k - 6) * math.pi / 36.0
        normal_x = jnp.where(sector == float(k), math.cos(angle), normal_x)
        normal_y = jnp.where(sector == float(k), math.sin(angle), normal_y)
    cell_x = lax.broadcasted_iota(jnp.int32, (NX, 128), 0).astype(F32)
    hot = jnp.where(cell_x == hub_x, 1.0, 0.0).astype(BF16)
    cell_y = lax.broadcasted_iota(jnp.int32, (NY, 128), 0)
    cell_y = jnp.where(cell_y > half, NY + half - cell_y, cell_y)
    off_y = cell_y.astype(F32) - hub_y
    off_z = (gz * 4 + gy).astype(F32) - hub_z
    disk = jnp.where(off_y * off_y + off_z * off_z <= float(RADIUS * RADIUS), 1.0, 0.0)

    def project(first, inflow):
        def column(index, mean):
            high, low = halves(phys[index] + mean)
            return dot(high, hot) + dot(low, hot)

        mixed = normal_x * column(first, inflow[0]) + normal_y * column(first + 1, inflow[1])
        return jnp.sum(disk * mixed, axis=0, keepdims=True)

    @pl.loop(0, 9)
    def _(task):
        @pl.when(task == 0)
        def _():
            drain_tiles(66, r2.at[5])

        @pl.when(task == 1)
        def _():
            flow_second(1)
            pull_second(7)
            drain_tiles(66, r2.at[6])

        @pl.when(task == 2)
        def _():
            curl(6, (5,))

        @pl.when(task == 3)
        def _():
            pull_second(9)
            send_visc()
            flow_first(3)
            flow_second(2)
            pull_first(4)
            drain_tiles(66, r2.at[7])
            drain_tiles(66, r2.at[8])
            curl(6, (3,))

        @pl.when(task == 5)
        def _():
            drain(plane.at[0], r2.at[0])

        @pl.when(task == 6)
        def _():
            drain_tiles(66, r2.at[9])
            curl(6, (4,))

        @pl.when(task == 7)
        def _():
            drain(plane.at[1], r2.at[1])

        @pl.when(task == 8)
        def _():
            part[...] = jnp.zeros((8, 128), F32)
            part[0:1, :] = project(0, (inflow_ref[0], inflow_ref[1]))
            part[1:2, :] = project(6, (0.0, 0.0))
            to_rings(lambda k: part, part_a.at[e], sa.at[0], ra.at[0])
            drain(plane.at[2], r2.at[2])

        slot = jnp.int32(0)
        for step, value in enumerate((6, 7, 11, 9, 8, 0, 10, 1, 2)):
            slot = jnp.where(task == step, value, slot)
        to_cells(slot)

    drain(visc, rv.at[0])
    first = lax.broadcasted_iota(jnp.int32, (half, half), 0)
    second = lax.broadcasted_iota(jnp.int32, (half, half), 1)
    swap = jnp.where((first + second) % half == 0, 1.0, 0.0).astype(BF16)
    high, low = halves(visc[half:])
    visc[half:] = dot(swap, high) + dot(swap, low)

    @pl.loop(0, 32)
    def _(block):
        at = octet(block)
        u0, u1, u2 = [phys[k, at] + inflow_ref[k] for k in range(3)]
        p0, p1, p2 = [phys[6 + k, at] for k in range(3)]
        q1, q0, q2 = [phys[9 + k, at] for k in range(3)]
        nu = visc[at]
        phys[9, at] = p1 * u2 - p2 * u1 - nu * q0
        phys[10, at] = p2 * u0 - p0 * u2 - nu * q1
        phys[11, at] = p0 * u1 - p1 * u0 - nu * q2

    flow_second(3)

    def to_modes(source, target):
        moved = halves(phys[source])
        for h in range(2):
            cols = pl.ds(h * 256, 256)
            spectrum = three(moved, (xf_ref[0, :, cols], xf_ref[1, :, cols]))
            top, low = spectrum[:half], spectrum[half:]
            even = jnp.where(edge, top, top + low)
            odd = jnp.where(edge, low, turn(low - top))
            done = three((yf_ref[0], yf_ref[1]), halves(jnp.concatenate([even, odd], 0)))
            plane[target, :, :, cols] = done.reshape(RINGS, 16, 256)

    def mine(ref, k):
        return ref.at[:, octet(k // 4), lanes(k % 4)]

    def sheet_first(k, slot, at):
        to_sheets(lambda other: plane.at[slot, other], fold.at[at, w], s3.at[k], r3.at[k])

    def sheet_second(k, at):
        drain(fold.at[at], r3.at[k])
        to_rings(lambda other: mine(fold.at[at], other), pencil.at[k, e], s4.at[k], r4.at[k])

    def ring_first(k, slot, at):
        to_rings(lambda other: mine(plane.at[slot], other), turned.at[at, e], s3.at[k], r3.at[k])

    def ring_second(k, at):
        drain(turned.at[at], r3.at[k])
        to_sheets(lambda other: turned.at[at, :, other], pencil.at[k, :, w], s4.at[k], r4.at[k])

    @pl.loop(0, 3)
    def _(j):
        to_modes(9 + j, 6 + j)

        @pl.when(j == 0)
        def _():
            ring_first(0, 6, 0)
            drain(part_a, ra.at[0])
            total = part_a[0]
            for k in range(1, RING):
                total = total + part_a[k]
            part_b[RINGS] = total
            to_sheets(lambda k: part_b.at[RINGS], part_b.at[w], sa.at[1], ra.at[1])
            last_second()

        @pl.when(j == 1)
        def _():
            sheet_first(1, 7, 0)

    curl(0, (5,))
    to_cells(5)
    drain(part_b.at[pl.ds(0, RINGS)], ra.at[1])
    total = part_b[0]
    for k in range(1, RINGS):
        total = total + part_b[k]
    disk_speed = total[0:1] / disk_area()
    push = total[1:2]
    grad = -0.5 * SECTION_STEP * disk_speed * jnp.abs(disk_speed) * push
    grad_ref[...] = grad[:, : grad_ref.shape[1]]
    weight = -thrust * jnp.abs(disk_speed) * push / disk_area()

    for index, normal in ((9, normal_x), (10, normal_y)):
        high, low = halves(disk * (weight * normal))
        phys[index] = dot_nt(high, hot) + dot_nt(low, hot)

    drain(plane.at[3], r2.at[3])
    curl(0, (3,))
    to_cells(3)

    @pl.loop(0, 32)
    def _(block):
        at = octet(block)
        phys[9, at] = phys[9, at] + phys[3, at] * phys[8, at] - phys[5, at] * phys[7, at]

    ring_second(0, 0)
    to_modes(9, 9)

    @pl.loop(0, RINGS)
    def _(block):
        plane[9, block] = plane[9, block] + wave_y_of(block) * turn(plane[8, block])

    ring_first(2, 9, 1)
    drain(plane.at[4], r2.at[4])
    curl(0, (4,))
    to_cells(4)

    @pl.loop(0, 32)
    def _(block):
        at = octet(block)
        w1, w0, w2 = [phys[3 + k, at] for k in range(3)]
        p0, p1, p2 = [phys[6 + k, at] for k in range(3)]
        phys[10, at] = phys[10, at] + w2 * p0 - w0 * p2
        phys[11, at] = w0 * p1 - w1 * p0

    @pl.loop(1, 3)
    def _(j):
        to_modes(9 + j, 9 + j)

        @pl.loop(0, RINGS)
        def _(block):
            own = plane[9 + j, block]

            @pl.when(j == 1)
            def _():
                plane[10, block] = own - wave_x * turn(plane[8, block])

            @pl.when(j == 2)
            def _():
                plane[11, block] = own + wave_x * turn(plane[7, block]) - wave_y_of(block) * turn(plane[6, block])

        @pl.when(j == 1)
        def _():
            sheet_first(3, 10, 1)
            sheet_second(1, 0)

        @pl.when(j == 2)
        def _():
            sheet_first(4, 11, 2)

    ring_second(2, 1)
    sheet_second(3, 1)
    sheet_second(4, 2)
    pencils = pencil.reshape(5, 1024, 128)

    def z_forward(f, table, fields):
        for pair in range(4):
            tall = []
            for k in fields:
                own = jnp.concatenate([pencils[k, pl.ds(2 * pair + i, 128, stride=8), :] for i in range(2)], 1)
                tall += [own, turn(own)]
            done = three(table, halves(jnp.concatenate(tall, 0)))
            for i in range(2):
                at = pl.ds(2 * pair + i, 128, stride=8)
                doubled = jnp.where(
                    (lax.broadcasted_iota(jnp.int32, (128, 1), 0) % WIDTH == 0) & (gy == 0), 1.0, 2.0
                )
                out_ref[f, at, :] = adj[f, at, :] * doubled + SECTION_STEP * done[:, i * 128 : i * 128 + 128].T

    for k in range(3):
        drain(pencil.at[k], r4.at[k])
    z_forward(0, (zf_ref[0, 0], zf_ref[1, 0]), (2, 1))
    drain(pencil.at[3], r4.at[3])
    z_forward(1, (zf_ref[0, 1], zf_ref[1, 1]), (3, 0))
    drain(pencil.at[4], r4.at[4])
    z_forward(2, (zf_ref[0, 0, :, :256], zf_ref[1, 0, :, :256]), (4,))

    for f in range(4):
        drain_tiles(112, s1.at[f])
        drain_tiles(120, s2.at[f])
    drain_tiles(120, s1.at[4])
    drain_tiles(112, s2.at[4])
    for k in range(5):
        drain_tiles(112 if k in (0, 2) else 120, s3.at[k])
        drain_tiles(120 if k in (0, 2) else 112, s4.at[k])

    @pl.when(kept)
    def _():
        for f in range(5, 10):
            drain_tiles(120, s1.at[f])

    @pl.when(kept_x)
    def _():
        for f in range(5, 10):
            drain_tiles(77, s2.at[f])

    drain(visc.at[pl.ds(0, 192)], sv.at[0])
    drain(part_a.at[pl.ds(0, RING - 1)], sa.at[0])
    drain(part_b.at[pl.ds(0, RINGS - 1)], sa.at[1])


def local(velocity_hat, inflow, viscosity, cot_hat, mode_mask, hub_cells, yaw_sector, thrust):
    count = thrust.shape[0]
    vmem = pl.BlockSpec(memory_space=pltpu.VMEM)
    smem = pl.BlockSpec(memory_space=pltpu.SMEM)
    dma = pltpu.SemaphoreType.DMA
    z_inverse, z_forward, y_inverse, y_forward, x_inverse, x_forward = [jnp.asarray(t) for t in tables()]
    operands = [
        cot_hat.reshape(3, 1024, 128), mode_mask.reshape(512, 128), z_inverse, velocity_hat.reshape(3, 1024, 128),
        y_inverse, x_inverse, x_forward, y_forward, z_forward,
    ]
    adjoint, grad = pl.pallas_call(
        kernel,
        out_shape=(
            jax.ShapeDtypeStruct((3, 1024, 128), F32),
            jax.ShapeDtypeStruct((1, count), F32),
        ),
        in_specs=[smem, vmem, vmem, vmem] + [pl.BlockSpec(memory_space=pl.ANY)] * 10,
        out_specs=(vmem, vmem),
        scratch_shapes=[pltpu.VMEM(each.shape, each.dtype) for each in operands] + [
            pltpu.VMEM((3, 1024, 128), F32),
            pltpu.VMEM((10, RING, RINGS, 8, 128), F32),
            pltpu.VMEM((4, RINGS, 16, NX), F32),
            pltpu.VMEM((6, RINGS, RING, 8, 128), F32),
            pltpu.VMEM((12, RINGS, 16, NX), F32),
            pltpu.VMEM((12, NY, NX), F32),
            pltpu.VMEM((NY, NX), F32),
            pltpu.VMEM((NY, NX), F32),
            pltpu.VMEM((3, RINGS, 16, NX), F32),
            pltpu.VMEM((2, RING, RINGS, 8, 128), F32),
            pltpu.VMEM((5, RING, RINGS, 8, 128), F32),
            pltpu.VMEM((8, 128), F32),
            pltpu.VMEM((RING, 8, 128), F32),
            pltpu.VMEM((RINGS + 1, 8, 128), F32),
            pltpu.VMEM((8, 128), F32),
            dma((10,)), dma((10,)), dma((10,)), dma((10,)),
            dma((5,)), dma((5,)), dma((5,)), dma((5,)),
            dma((1,)), dma((1,)), dma((2,)), dma((2,)), dma((9,)),
        ],
        compiler_params=pltpu.CompilerParams(
            collective_id=0, has_side_effects=True, vmem_limit_bytes=60 * 1024 * 1024
        ),
    )(
        inflow,
        hub_cells.T,
        yaw_sector.reshape(1, count),
        thrust.reshape(1, count),
        viscosity,
        *operands,
    )
    return adjoint.reshape(velocity_hat.shape), grad.reshape(count)


def solution(mesh):
    placed = (
        P(None, None, "gy", "gz", None),
        P(),
        P("gz", "gy", None),
        P(None, None, "gy", "gz", None),
        P("gy", "gz", None),
        P(),
        P(),
        P(),
    )
    return jax.shard_map(
        local,
        mesh=mesh,
        in_specs=placed,
        out_specs=(P(None, None, "gy", "gz", None), P()),
        check_vma=False,
    )
```

```python
import math

import jax
import jax.numpy as jnp
import ml_dtypes
import numpy as np
from jax import lax
from jax.experimental import pallas as pl
from jax.experimental.pallas import tpu as pltpu
from jax.sharding import PartitionSpec as P

MESH = pl.DeviceIdType.MESH
F32 = jnp.float32
BF16 = jnp.bfloat16
RADIUS = 4
SECTION_STEP = 0.24
NX, NY, NZ = 512, 256, 128
WIDTH = 64
RING, RINGS = 8, 16


def disk_area():
    reach = range(-RADIUS, RADIUS + 1)
    return float(sum(1 for a in reach for b in reach if a * a + b * b <= RADIUS * RADIUS))


def signed(index, length):
    return np.where(index < length // 2, index, index - length)


def split(table):
    high = table.astype(ml_dtypes.bfloat16)
    low = (table - high.astype(np.float64)).astype(ml_dtypes.bfloat16)
    return np.stack([high, low])


def tables():
    e, w = np.meshgrid(np.arange(RING), np.arange(RINGS), indexing="ij")
    cell_z = ((w // 4) * 32 + (e // 4) * 16 + (w % 4) * 4 + e % 4).reshape(-1)
    mode_z = np.arange(NZ)
    wave_z = 2.0 * math.pi / NZ * signed(mode_z, NZ)
    angle = 2.0 * math.pi / NZ * (cell_z[:, None] * mode_z[None, :] % NZ)
    cos, sin = np.cos(angle), np.sin(angle)
    z_inverse = np.block([[cos, sin], [-wave_z * sin, wave_z * cos]])
    cos, sin = cos.T, sin.T
    wave_z = wave_z[:, None]
    z_first = np.block([cos, -sin, -wave_z * sin, -wave_z * cos])
    z_second = np.block([cos, -sin, wave_z * sin, wave_z * cos])
    row = np.arange(NY)
    w, z_lo, r = row // 16, row // 8 % 2, row % 8
    mode_y = (w // 4) * 64 + z_lo * 32 + (w % 4) * 8 + r
    angle = 2.0 * math.pi / NY * (np.arange(NY // 2 + 1)[:, None] * mode_y[None, :] % NY)
    cos, sin = np.cos(angle), np.sin(angle)
    y_inverse = np.concatenate([cos, sin[1 : NY // 2]])
    lane = np.arange(NX)
    mode_x = lane // 128 * WIDTH + lane % WIDTH
    weight = np.where(mode_x == 0, 1.0, 2.0) / math.sqrt(NX * NY * NZ)
    angle = 2.0 * math.pi / NX * (mode_x[:, None] * np.arange(NX)[None, :] % NX)
    real = (lane % 128 < WIDTH)[:, None]
    x_inverse = weight[:, None] * np.where(real, np.cos(angle), -np.sin(angle))
    return [split(t) for t in (z_inverse, np.stack([z_first, z_second]), y_inverse, y_inverse.T, x_inverse, x_inverse.T)]


def halves(value):
    high = value.astype(BF16)
    return high, (value - high.astype(F32)).astype(BF16)


def dot(left, right):
    return jnp.dot(left, right, preferred_element_type=F32)


def dot_nt(left, right):
    return lax.dot_general(left, right, (((1,), (1,)), ((), ())), preferred_element_type=F32)


def three(left, right, product=dot):
    return product(left[0], right[0]) + product(left[0], right[1]) + product(left[1], right[0])


def kernel(
    inflow_ref, hub_ref, sector_ref, thrust_ref, visc_ref, *refs,
):
    held, refs = refs[:9], refs[9:]
    (out_ref, grad_ref), refs = refs[:2], refs[2:]
    loaded, refs = refs[:9], refs[9:]
    cot_ref, mask_ref, zi_ref, modes_ref, yi_ref, xi_ref, xf_ref, yf_ref, zf_ref = loaded
    (
        adj, sent, ring, sheet, plane, phys, visc, rows, fold, turned, pencil, result, part, part_a, part_b, turbine,
        s1, r1, s2, r2, s3, r3, s4, r4, sv, rv, sa, ra, load, leave,
    ) = refs
    gy = lax.axis_index("gy")
    gz = lax.axis_index("gz")
    x = gz // 8
    z_lo = gz // 4 % 2
    y = gz % 4
    z = gy // 2 * 2 + z_lo
    core = gy % 2
    e = z_lo * 4 + gy
    w = x * 4 + y
    kept_x = gy < 3
    kept = kept_x & ((gz < 11) | (gz > 20))

    def ring_id(other):
        return {"gy": other % 4, "gz": x * 8 + other // 4 * 4 + y}

    def sheet_id(other):
        return {"gy": gy, "gz": other // 4 * 8 + z_lo * 4 + other % 4}

    def to_ring(step):
        turn = step * 3 % RING
        there = (z + turn) % 4
        return there % 2 * 4 + there // 2 * 2 + (core + turn // 4) % 2

    def to_sheet(step):
        turn = step * 5 % RINGS
        return (x + turn // 4) % 4 * 4 + (y + turn) % 4

    barrier = pltpu.get_barrier_semaphore()

    @pl.loop(1, RING)
    def _(step):
        pl.semaphore_signal(barrier, inc=1, device_id=ring_id(to_ring(step)), device_id_type=MESH)

    @pl.loop(1, RINGS)
    def _(step):
        pl.semaphore_signal(barrier, inc=1, device_id=sheet_id(to_sheet(step)), device_id_type=MESH)

    loads = [pltpu.make_async_copy(held[k], loaded[k], load.at[k]) for k in range(9)]
    for copy in loads:
        copy.start()

    def exchange(steps, target, device, source, landing, send, receive):
        @pl.loop(1, steps)
        def _(step):
            other = target(step)
            pltpu.make_async_remote_copy(
                src_ref=source(other), dst_ref=landing, send_sem=send, recv_sem=receive,
                device_id=device(other), device_id_type=MESH,
            ).start()

        pltpu.make_async_copy(source(target(0)), landing, receive).start()

    def to_rings(source, landing, send, receive):
        exchange(RING, to_ring, ring_id, source, landing, send, receive)

    def to_sheets(source, landing, send, receive):
        exchange(RINGS, to_sheet, sheet_id, source, landing, send, receive)

    def drain(ref, sem):
        pltpu.make_async_copy(ref, ref, sem).wait()

    tiles = sent.reshape(1280, 8, 128)

    def drain_tiles(count, sem):
        drain(tiles.at[pl.ds(0, count)], sem)

    def lanes(index):
        return pl.ds(pl.multiple_of(index * 128, 128), 128)

    def octet(index):
        return pl.ds(pl.multiple_of(index * 8, 8), 8)

    def tile_waves(kx):
        wave_x = (2.0 * math.pi / NX) * (gy * WIDTH + kx).astype(F32)
        iy = gz * 8 + lax.broadcasted_iota(jnp.int32, (8, 128), 0)
        iz = lax.broadcasted_iota(jnp.int32, (8, 128), 1)
        wave_y = (2.0 * math.pi / NY) * jnp.where(iy < NY // 2, iy, iy - NY).astype(F32)
        wave_z = (2.0 * math.pi / NZ) * jnp.where(iz < NZ // 2, iz, iz - NZ).astype(F32)
        return wave_x, wave_y, wave_z

    loads[0].wait()
    loads[1].wait()

    @pl.loop(0, WIDTH)
    def _(kx):
        wave_x, wave_y, wave_z = tile_waves(kx)
        square = wave_x * wave_x + wave_y * wave_y + wave_z * wave_z
        inverse = jnp.where(square > 0, 1.0, 0.0) / jnp.where(square > 0, square, 1.0)
        first = octet(kx)
        scale = mask_ref[first, :].astype(F32) * jnp.where(gy * WIDTH + kx == 0, 1.0, 0.5)
        for c in range(2):
            at = octet(c * WIDTH + kx)
            v0, v1, v2 = cot_ref[0, at, :], cot_ref[1, at, :], cot_ref[2, at, :]
            along = (wave_x * v0 + wave_y * v1 + wave_z * v2) * inverse
            adj[0, at, :] = scale * (v0 - wave_x * along)
            adj[1, at, :] = scale * (v1 - wave_y * along)
            adj[2, at, :] = scale * (v2 - wave_z * along)

    def z_inverse(source, f, base):
        table = (zi_ref[0], zi_ref[1])
        view = sent.reshape(10, 1024, 128)
        for pair in range(4):
            wide = []
            for ky in (2 * pair, 2 * pair + 1):
                own = source[f, pl.ds(ky, 128, stride=8), :]
                wide.append(jnp.concatenate([own, jnp.concatenate([-own[64:], own[:64]], 0)], 1))
            done = three(table, halves(jnp.concatenate(wide, 0)), dot_nt)
            for k in range(2):
                at = pl.ds(2 * pair + k, 128, stride=8)
                view[base + f, at, :] = done[:128, k * 128 : k * 128 + 128]

                @pl.when(f < 2)
                def _():
                    view[base + 3 + f, at, :] = done[128:, k * 128 : k * 128 + 128]

    def flow_first(f):
        to_rings(lambda k: sent.at[f, k], ring.at[f, :, octet(z_lo), lanes(gy)], s1.at[f], r1.at[f])

    def flow_second(f):
        drain(ring.at[f], r1.at[f])
        to_sheets(lambda k: ring.at[f, k], plane.at[f, w], s2.at[f], r2.at[f])

    def pull_first(f):
        to_sheets(lambda k: sent.at[f, :, k], sheet.at[f - 4, w], s1.at[f], r1.at[f])

    def last_second():
        drain(sheet.at[0], r1.at[4])
        to_rings(lambda k: sheet.at[0, :, k], plane.at[4, :, octet(z_lo), lanes(gy)], s2.at[4], r2.at[4])

    def pull_second(f):
        @pl.when(kept_x)
        def _():
            drain_tiles(88, r1.at[f])
            for first, count in ((0, 4), (4 + 5 * z_lo, 3), (12, 4)):
                some = pl.ds(first, count)
                to_rings(
                    lambda k: sheet.at[f - 4, some, k], plane.at[f + 1, some, octet(z_lo), lanes(gy)],
                    s2.at[f], r2.at[f],
                )

    def send_visc():
        landing = visc.at[pl.ds(pl.multiple_of(gy * 64, 64), 64)]

        @pl.loop(1, 4)
        def _(step):
            other = (gy + step) % 4
            pltpu.make_async_remote_copy(
                src_ref=visc_ref.at[other], dst_ref=landing, send_sem=sv.at[0], recv_sem=rv.at[0],
                device_id={"gy": other, "gz": gz}, device_id_type=MESH,
            ).start()

        pltpu.make_async_copy(visc_ref.at[gy], landing, rv.at[0]).start()

    def pull_fields(f):
        pull_first(5 + f)

        @pl.when(f == 0)
        def _():
            pull_first(8)

        @pl.when(f == 2)
        def _():
            pull_first(9)

    loads[2].wait()

    @pl.when(kept)
    def _():
        z_inverse(adj, 0, 5)

    loads[3].wait()
    z_inverse(modes_ref, 0, 0)
    pl.semaphore_wait(barrier, RING + RINGS - 2)

    @pl.when(kept)
    def _():
        pull_fields(0)

    flow_first(0)
    @pl.loop(1, 3)
    def _(f):
        @pl.when(kept)
        def _():
            z_inverse(adj, f, 5)
            pull_fields(f)

        z_inverse(modes_ref, f, 0)

        @pl.when(f == 1)
        def _():
            flow_first(1)

    @pl.loop(6, 11)
    def _(slot):
        plane[slot, :, :, 384:] = jnp.zeros((RINGS, 16, 128), F32)
        plane[slot, 4:7, 8:, :384] = jnp.zeros((3, 8, 384), F32)
        plane[slot, 7:9, :, :384] = jnp.zeros((2, 16, 384), F32)
        plane[slot, 9:12, :8, :384] = jnp.zeros((3, 8, 384), F32)

    pull_second(5)
    pull_second(8)
    flow_second(0)
    pull_second(6)
    flow_first(2)
    for copy in loads[4:]:
        copy.wait()

    lane = lax.broadcasted_iota(jnp.int32, (1, NX), 1)
    wave_x = (2.0 * math.pi / NX) * ((lane // 128) * WIDTH + lane % WIDTH).astype(F32)
    sign = jnp.where(lane % 128 < WIDTH, -1.0, 1.0).astype(F32)

    def turn(value):
        parts = [pltpu.roll(value[:, k * 128 : k * 128 + 128], 64, 1) for k in range(value.shape[1] // 128)]
        return jnp.concatenate(parts, 1) * sign[:, : value.shape[1]]

    def wave_y_of(block):
        row = lax.broadcasted_iota(jnp.int32, (16, 1), 0)
        mode = (block // 4) * 64 + (block % 4) * 8 + (row // 8) * 32 + row % 8
        return (2.0 * math.pi / NY) * jnp.where(mode < NY // 2, mode, mode - NY).astype(F32)

    def curl(base, slots):
        @pl.loop(0, RINGS)
        def _(block):
            wave_y = wave_y_of(block)
            if 3 in slots:
                plane[base + 3, block] = plane[base + 3, block] - wave_x * turn(plane[base + 2, block])
            if 4 in slots:
                plane[base + 4, block] = wave_y * turn(plane[base + 2, block]) - plane[base + 4, block]
            if 5 in slots:
                plane[base + 5, block] = wave_x * turn(plane[base + 1, block]) - wave_y * turn(plane[base, block])

    half = NY // 2
    edge = lax.broadcasted_iota(jnp.int32, (half, 256), 0) == 0

    def to_cells(index):
        for h in range(2):
            cols = pl.ds(h * 256, 256)
            both = three((yi_ref[0], yi_ref[1]), halves(plane[index, :, :, cols].reshape(NY, 256)))
            top, low = both[:half], both[half:]
            spun = turn(low)
            rows[:half, cols] = jnp.where(edge, top, top + spun)
            rows[half:, cols] = jnp.where(edge, low, top - spun)
        moved = halves(rows[...])
        for h in range(2):
            cols = pl.ds(h * 256, 256)
            done = three(moved, (xi_ref[0, :, cols], xi_ref[1, :, cols]))
            phys[index, :, cols] = done

    count = thrust_ref.shape[1]
    turbine[...] = jnp.full((8, 128), -1000.0, F32)
    turbine[0:3, :count] = hub_ref[...].astype(F32)
    turbine[3:4, :count] = sector_ref[...].astype(F32)
    turbine[4:5, :count] = thrust_ref[...]
    hub_x, hub_y, hub_z, sector, thrust = [turbine[k : k + 1, :] for k in range(5)]
    normal_x = normal_y = jnp.zeros((1, 128), F32)
    for k in range(13):
        angle = (k - 6) * math.pi / 36.0
        normal_x = jnp.where(sector == float(k), math.cos(angle), normal_x)
        normal_y = jnp.where(sector == float(k), math.sin(angle), normal_y)
    cell_x = lax.broadcasted_iota(jnp.int32, (NX, 128), 0).astype(F32)
    hot = jnp.where(cell_x == hub_x, 1.0, 0.0).astype(BF16)
    cell_y = lax.broadcasted_iota(jnp.int32, (NY, 128), 0)
    cell_y = jnp.where(cell_y > half, NY + half - cell_y, cell_y)
    off_y = cell_y.astype(F32) - hub_y
    off_z = (gz * 4 + gy).astype(F32) - hub_z
    disk = jnp.where(off_y * off_y + off_z * off_z <= float(RADIUS * RADIUS), 1.0, 0.0)

    def project(first, inflow):
        def column(index, mean):
            high, low = halves(phys[index] + mean)
            return dot(high, hot) + dot(low, hot)

        mixed = normal_x * column(first, inflow[0]) + normal_y * column(first + 1, inflow[1])
        return jnp.sum(disk * mixed, axis=0, keepdims=True)

    @pl.loop(0, 9)
    def _(task):
        @pl.when(task == 0)
        def _():
            drain_tiles(66, r2.at[5])

        @pl.when(task == 1)
        def _():
            flow_second(1)
            pull_second(7)
            drain_tiles(66, r2.at[6])

        @pl.when(task == 2)
        def _():
            curl(6, (5,))

        @pl.when(task == 3)
        def _():
            pull_second(9)
            send_visc()
            flow_first(3)
            flow_second(2)
            pull_first(4)
            drain_tiles(66, r2.at[7])
            drain_tiles(66, r2.at[8])
            curl(6, (3,))

        @pl.when(task == 5)
        def _():
            drain(plane.at[0], r2.at[0])

        @pl.when(task == 6)
        def _():
            drain_tiles(66, r2.at[9])
            curl(6, (4,))

        @pl.when(task == 7)
        def _():
            drain(plane.at[1], r2.at[1])

        @pl.when(task == 8)
        def _():
            part[...] = jnp.zeros((8, 128), F32)
            part[0:1, :] = project(0, (inflow_ref[0], inflow_ref[1]))
            part[1:2, :] = project(6, (0.0, 0.0))
            to_rings(lambda k: part, part_a.at[e], sa.at[0], ra.at[0])
            drain(plane.at[2], r2.at[2])

        slot = jnp.int32(0)
        for step, value in enumerate((6, 7, 11, 9, 8, 0, 10, 1, 2)):
            slot = jnp.where(task == step, value, slot)
        to_cells(slot)

    drain(visc, rv.at[0])
    first = lax.broadcasted_iota(jnp.int32, (half, half), 0)
    second = lax.broadcasted_iota(jnp.int32, (half, half), 1)
    swap = jnp.where((first + second) % half == 0, 1.0, 0.0).astype(BF16)
    high, low = halves(visc[half:])
    visc[half:] = dot(swap, high) + dot(swap, low)

    @pl.loop(0, 32)
    def _(block):
        at = octet(block)
        u0, u1, u2 = [phys[k, at] + inflow_ref[k] for k in range(3)]
        p0, p1, p2 = [phys[6 + k, at] for k in range(3)]
        q1, q0, q2 = [phys[9 + k, at] for k in range(3)]
        nu = visc[at]
        phys[9, at] = p1 * u2 - p2 * u1 - nu * q0
        phys[10, at] = p2 * u0 - p0 * u2 - nu * q1
        phys[11, at] = p0 * u1 - p1 * u0 - nu * q2

    flow_second(3)

    def to_modes(source, target, extra=None):
        moved = halves(phys[source])
        for h in range(2):
            cols = pl.ds(h * 256, 256)
            spectrum = three(moved, (xf_ref[0, :, cols], xf_ref[1, :, cols]))
            top, low = spectrum[:half], spectrum[half:]
            even = jnp.where(edge, top, top + low)
            odd = jnp.where(edge, low, turn(low - top))
            done = three((yf_ref[0], yf_ref[1]), halves(jnp.concatenate([even, odd], 0)))
            if extra is not None:
                done = done + extra(cols)
            plane[target, :, :, cols] = done.reshape(RINGS, 16, 256)

    def mine(ref, k):
        return ref.at[:, octet(k // 4), lanes(k % 4)]

    def sheet_first(k, slot, at):
        to_sheets(lambda other: plane.at[slot, other], fold.at[at, w], s3.at[k], r3.at[k])

    def sheet_second(k, at):
        drain(fold.at[at], r3.at[k])
        to_rings(lambda other: mine(fold.at[at], other), pencil.at[k, e], s4.at[k], r4.at[k])

    def ring_first(k, slot, at):
        to_rings(lambda other: mine(plane.at[slot], other), turned.at[at, e], s3.at[k], r3.at[k])

    def ring_second(k, at):
        drain(turned.at[at], r3.at[k])
        to_sheets(lambda other: turned.at[at, :, other], pencil.at[k, :, w], s4.at[k], r4.at[k])

    @pl.loop(0, 3)
    def _(j):
        to_modes(9 + j, 6 + j)

        @pl.when(j == 0)
        def _():
            ring_first(0, 6, 0)
            drain(part_a, ra.at[0])
            total = part_a[0]
            for k in range(1, RING):
                total = total + part_a[k]
            part_b[RINGS] = total
            to_sheets(lambda k: part_b.at[RINGS], part_b.at[w], sa.at[1], ra.at[1])
            last_second()

        @pl.when(j == 1)
        def _():
            sheet_first(1, 7, 0)

    curl(0, (5,))
    to_cells(5)
    drain(part_b.at[pl.ds(0, RINGS)], ra.at[1])
    total = part_b[0]
    for k in range(1, RINGS):
        total = total + part_b[k]
    disk_speed = total[0:1] / disk_area()
    push = total[1:2]
    grad = -0.5 * SECTION_STEP * disk_speed * jnp.abs(disk_speed) * push
    grad_ref[...] = grad[:, : grad_ref.shape[1]]
    weight = -thrust * jnp.abs(disk_speed) * push / disk_area()

    for index, normal in ((9, normal_x), (10, normal_y)):
        high, low = halves(disk * (weight * normal))
        phys[index] = dot_nt(high, hot) + dot_nt(low, hot)

    drain(plane.at[3], r2.at[3])
    curl(0, (3,))
    to_cells(3)

    @pl.loop(0, 32)
    def _(block):
        at = octet(block)
        phys[9, at] = phys[9, at] + phys[3, at] * phys[8, at] - phys[5, at] * phys[7, at]

    ring_second(0, 0)
    spread_y = jnp.concatenate([wave_y_of(block) for block in range(RINGS)], 0)

    def spun(slot, cols):
        return turn(plane[slot, :, :, cols].reshape(NY, 256))

    def across(cols):
        return wave_x[:, cols.start : cols.start + 256]

    to_modes(9, 9, lambda cols: spread_y * spun(8, cols))
    ring_first(2, 9, 1)
    drain(plane.at[4], r2.at[4])
    curl(0, (4,))
    to_cells(4)

    @pl.loop(0, 32)
    def _(block):
        at = octet(block)
        w1, w0, w2 = [phys[3 + k, at] for k in range(3)]
        p0, p1, p2 = [phys[6 + k, at] for k in range(3)]
        phys[10, at] = phys[10, at] + w2 * p0 - w0 * p2
        phys[11, at] = w0 * p1 - w1 * p0

    to_modes(10, 10, lambda cols: -across(cols) * spun(8, cols))
    sheet_first(3, 10, 1)
    sheet_second(1, 0)
    to_modes(11, 11, lambda cols: across(cols) * spun(7, cols) - spread_y * spun(6, cols))
    sheet_first(4, 11, 2)
    ring_second(2, 1)
    sheet_second(3, 1)
    sheet_second(4, 2)
    pencils = pencil.reshape(5, 1024, 128)

    def z_forward(f, table, fields):
        for pair in range(4):
            tall = []
            for k in fields:
                own = jnp.concatenate([pencils[k, pl.ds(2 * pair + i, 128, stride=8), :] for i in range(2)], 1)
                tall += [own, turn(own)]
            done = three(table, halves(jnp.concatenate(tall, 0)))
            for i in range(2):
                at = pl.ds(2 * pair + i, 128, stride=8)
                doubled = jnp.where(
                    (lax.broadcasted_iota(jnp.int32, (128, 1), 0) % WIDTH == 0) & (gy == 0), 1.0, 2.0
                )
                result[f, at, :] = adj[f, at, :] * doubled + SECTION_STEP * done[:, i * 128 : i * 128 + 128].T

        pltpu.make_async_copy(result.at[f], out_ref.at[f], leave.at[f]).start()

    for k in range(3):
        drain(pencil.at[k], r4.at[k])
    z_forward(0, (zf_ref[0, 0], zf_ref[1, 0]), (2, 1))
    drain(pencil.at[3], r4.at[3])
    z_forward(1, (zf_ref[0, 1], zf_ref[1, 1]), (3, 0))
    drain(pencil.at[4], r4.at[4])
    z_forward(2, (zf_ref[0, 0, :, :256], zf_ref[1, 0, :, :256]), (4,))

    for f in range(4):
        drain_tiles(112, s1.at[f])
        drain_tiles(120, s2.at[f])
    drain_tiles(120, s1.at[4])
    drain_tiles(112, s2.at[4])
    for k in range(5):
        drain_tiles(112 if k in (0, 2) else 120, s3.at[k])
        drain_tiles(120 if k in (0, 2) else 112, s4.at[k])

    @pl.when(kept)
    def _():
        for f in range(5, 10):
            drain_tiles(120, s1.at[f])

    @pl.when(kept_x)
    def _():
        for f in range(5, 10):
            drain_tiles(77, s2.at[f])

    for f in range(3):
        pltpu.make_async_copy(result.at[f], out_ref.at[f], leave.at[f]).wait()
    drain(visc.at[pl.ds(0, 192)], sv.at[0])
    drain(part_a.at[pl.ds(0, RING - 1)], sa.at[0])
    drain(part_b.at[pl.ds(0, RINGS - 1)], sa.at[1])


def carry(adjoint, grad, adjoint_out, grad_out, rest, small, arrive, leave):
    pieces = [(adjoint.at[f, pl.ds(k * 512, 512)], rest.at[f, pl.ds(k * 512, 512)], adjoint_out.at[f, pl.ds(k * 512, 512)])
              for f in range(3) for k in range(2)]
    pieces.append((grad, small, grad_out))
    inward = [pltpu.make_async_copy(piece[0], piece[1], arrive.at[k]) for k, piece in enumerate(pieces)]
    outward = [pltpu.make_async_copy(piece[1], piece[2], leave.at[k]) for k, piece in enumerate(pieces)]
    for copy in inward:
        copy.start()
    for first, then in zip(inward, outward):
        first.wait()
        then.start()
    for copy in outward:
        copy.wait()


def local(velocity_hat, inflow, viscosity, cot_hat, mode_mask, hub_cells, yaw_sector, thrust):
    count = thrust.shape[0]
    vmem = pl.BlockSpec(memory_space=pltpu.VMEM)
    smem = pl.BlockSpec(memory_space=pltpu.SMEM)
    dma = pltpu.SemaphoreType.DMA
    z_inverse, z_forward, y_inverse, y_forward, x_inverse, x_forward = [jnp.asarray(t) for t in tables()]
    operands = [
        cot_hat.reshape(3, 1024, 128), mode_mask.reshape(512, 128), z_inverse, velocity_hat.reshape(3, 1024, 128),
        y_inverse, x_inverse, x_forward, y_forward, z_forward,
    ]
    adjoint, grad = pl.pallas_call(
        kernel,
        out_shape=(
            jax.ShapeDtypeStruct((3, 1024, 128), F32),
            jax.ShapeDtypeStruct((1, count), F32),
        ),
        in_specs=[smem, vmem, vmem, vmem] + [pl.BlockSpec(memory_space=pl.ANY)] * 10,
        out_specs=(pl.BlockSpec(memory_space=pl.ANY), vmem),
        scratch_shapes=[pltpu.VMEM(each.shape, each.dtype) for each in operands] + [
            pltpu.VMEM((3, 1024, 128), F32),
            pltpu.VMEM((10, RING, RINGS, 8, 128), F32),
            pltpu.VMEM((4, RINGS, 16, NX), F32),
            pltpu.VMEM((6, RINGS, RING, 8, 128), F32),
            pltpu.VMEM((12, RINGS, 16, NX), F32),
            pltpu.VMEM((12, NY, NX), F32),
            pltpu.VMEM((NY, NX), F32),
            pltpu.VMEM((NY, NX), F32),
            pltpu.VMEM((3, RINGS, 16, NX), F32),
            pltpu.VMEM((2, RING, RINGS, 8, 128), F32),
            pltpu.VMEM((5, RING, RINGS, 8, 128), F32),
            pltpu.VMEM((3, 1024, 128), F32),
            pltpu.VMEM((8, 128), F32),
            pltpu.VMEM((RING, 8, 128), F32),
            pltpu.VMEM((RINGS + 1, 8, 128), F32),
            pltpu.VMEM((8, 128), F32),
            dma((10,)), dma((10,)), dma((10,)), dma((10,)),
            dma((5,)), dma((5,)), dma((5,)), dma((5,)),
            dma((1,)), dma((1,)), dma((2,)), dma((2,)), dma((9,)), dma((3,)),
        ],
        compiler_params=pltpu.CompilerParams(
            collective_id=0, has_side_effects=True, vmem_limit_bytes=60 * 1024 * 1024
        ),
    )(
        inflow,
        hub_cells.T,
        yaw_sector.reshape(1, count),
        thrust.reshape(1, count),
        viscosity,
        *operands,
    )
    whole = pl.BlockSpec(memory_space=pl.ANY)
    adjoint, grad = pl.pallas_call(
        carry,
        out_shape=tuple(jax.ShapeDtypeStruct(each.shape, F32) for each in (adjoint, grad)),
        in_specs=[whole, whole],
        out_specs=(whole, whole),
        scratch_shapes=[pltpu.VMEM(adjoint.shape, F32), pltpu.VMEM(grad.shape, F32), dma((7,)), dma((7,))],
    )(adjoint, grad)
    return adjoint.reshape(velocity_hat.shape), grad.reshape(count)


def solution(mesh):
    placed = (
        P(None, None, "gy", "gz", None),
        P(),
        P("gz", "gy", None),
        P(None, None, "gy", "gz", None),
        P("gy", "gz", None),
        P(),
        P(),
        P(),
    )
    return jax.shard_map(
        local,
        mesh=mesh,
        in_specs=placed,
        out_specs=(P(None, None, "gy", "gz", None), P()),
        check_vma=False,
    )
```

```python
import math

import jax
import jax.numpy as jnp
import ml_dtypes
import numpy as np
from jax import lax
from jax.experimental import pallas as pl
from jax.experimental.pallas import tpu as pltpu
from jax.sharding import PartitionSpec as P

MESH = pl.DeviceIdType.MESH
F32 = jnp.float32
BF16 = jnp.bfloat16
RADIUS = 4
SECTION_STEP = 0.24
NX, NY, NZ = 512, 256, 128
WIDTH = 64
RING, RINGS = 8, 16


def disk_area():
    reach = range(-RADIUS, RADIUS + 1)
    return float(sum(1 for a in reach for b in reach if a * a + b * b <= RADIUS * RADIUS))


def signed(index, length):
    return np.where(index < length // 2, index, index - length)


def split(table):
    high = table.astype(ml_dtypes.bfloat16)
    low = (table - high.astype(np.float64)).astype(ml_dtypes.bfloat16)
    return np.stack([high, low])


def tables():
    e, w = np.meshgrid(np.arange(RING), np.arange(RINGS), indexing="ij")
    cell_z = ((w // 4) * 32 + (e // 4) * 16 + (w % 4) * 4 + e % 4).reshape(-1)
    mode_z = np.arange(NZ)
    wave_z = 2.0 * math.pi / NZ * signed(mode_z, NZ)
    angle = 2.0 * math.pi / NZ * (cell_z[:, None] * mode_z[None, :] % NZ)
    cos, sin = np.cos(angle), np.sin(angle)
    z_inverse = np.block([[cos, sin], [-wave_z * sin, wave_z * cos]])
    cos, sin = cos.T, sin.T
    wave_z = wave_z[:, None]
    z_first = np.block([cos, -sin, -wave_z * sin, -wave_z * cos])
    z_second = np.block([cos, -sin, wave_z * sin, wave_z * cos])
    row = np.arange(NY)
    w, z_lo, r = row // 16, row // 8 % 2, row % 8
    mode_y = (w // 4) * 64 + z_lo * 32 + (w % 4) * 8 + r
    angle = 2.0 * math.pi / NY * (np.arange(NY // 2 + 1)[:, None] * mode_y[None, :] % NY)
    cos, sin = np.cos(angle), np.sin(angle)
    y_inverse = np.concatenate([cos, sin[1 : NY // 2]])
    lane = np.arange(NX)
    mode_x = lane // 128 * WIDTH + lane % WIDTH
    weight = np.where(mode_x == 0, 1.0, 2.0) / math.sqrt(NX * NY * NZ)
    angle = 2.0 * math.pi / NX * (mode_x[:, None] * np.arange(NX)[None, :] % NX)
    real = (lane % 128 < WIDTH)[:, None]
    x_inverse = weight[:, None] * np.where(real, np.cos(angle), -np.sin(angle))
    return [split(t) for t in (z_inverse, np.stack([z_first, z_second]), y_inverse, y_inverse.T, x_inverse, x_inverse.T)]


def halves(value):
    high = value.astype(BF16)
    return high, (value - high.astype(F32)).astype(BF16)


def dot(left, right):
    return jnp.dot(left, right, preferred_element_type=F32)


def dot_nt(left, right):
    return lax.dot_general(left, right, (((1,), (1,)), ((), ())), preferred_element_type=F32)


def three(left, right, product=dot):
    return product(left[0], right[0]) + product(left[0], right[1]) + product(left[1], right[0])


def kernel(
    inflow_ref, hub_ref, sector_ref, thrust_ref, visc_ref, *refs,
):
    held, refs = refs[:9], refs[9:]
    (out_ref, grad_ref), refs = refs[:2], refs[2:]
    loaded, refs = refs[:9], refs[9:]
    cot_ref, mask_ref, zi_ref, modes_ref, yi_ref, xi_ref, xf_ref, yf_ref, zf_ref = loaded
    (
        adj, sent, ring, sheet, plane, phys, visc, rows, fold, turned, pencil, result, part, part_a, part_b, turbine,
        s1, r1, s2, r2, s3, r3, s4, r4, sv, rv, sa, ra, load, leave,
    ) = refs
    gy = lax.axis_index("gy")
    gz = lax.axis_index("gz")
    x = gz // 8
    z_lo = gz // 4 % 2
    y = gz % 4
    z = gy // 2 * 2 + z_lo
    core = gy % 2
    e = z_lo * 4 + gy
    w = x * 4 + y
    kept_x = gy < 3
    kept = kept_x & ((gz < 11) | (gz > 20))

    def ring_id(other):
        return {"gy": other % 4, "gz": x * 8 + other // 4 * 4 + y}

    def sheet_id(other):
        return {"gy": gy, "gz": other // 4 * 8 + z_lo * 4 + other % 4}

    def to_ring(step):
        turn = step * 3 % RING
        there = (z + turn) % 4
        return there % 2 * 4 + there // 2 * 2 + (core + turn // 4) % 2

    def to_sheet(step):
        turn = step * 5 % RINGS
        return (x + turn // 4) % 4 * 4 + (y + turn) % 4

    barrier = pltpu.get_barrier_semaphore()

    @pl.loop(1, RING)
    def _(step):
        pl.semaphore_signal(barrier, inc=1, device_id=ring_id(to_ring(step)), device_id_type=MESH)

    @pl.loop(1, RINGS)
    def _(step):
        pl.semaphore_signal(barrier, inc=1, device_id=sheet_id(to_sheet(step)), device_id_type=MESH)

    loads = [pltpu.make_async_copy(held[k], loaded[k], load.at[k]) for k in range(9)]
    for copy in loads:
        copy.start()

    def exchange(steps, target, device, source, landing, send, receive):
        @pl.loop(1, steps)
        def _(step):
            other = target(step)
            pltpu.make_async_remote_copy(
                src_ref=source(other), dst_ref=landing, send_sem=send, recv_sem=receive,
                device_id=device(other), device_id_type=MESH,
            ).start()

        pltpu.make_async_copy(source(target(0)), landing, receive).start()

    def to_rings(source, landing, send, receive):
        exchange(RING, to_ring, ring_id, source, landing, send, receive)

    def to_sheets(source, landing, send, receive):
        exchange(RINGS, to_sheet, sheet_id, source, landing, send, receive)

    def drain(ref, sem):
        pltpu.make_async_copy(ref, ref, sem).wait()

    tiles = sent.reshape(1280, 8, 128)

    def drain_tiles(count, sem):
        drain(tiles.at[pl.ds(0, count)], sem)

    def lanes(index):
        return pl.ds(pl.multiple_of(index * 128, 128), 128)

    def octet(index):
        return pl.ds(pl.multiple_of(index * 8, 8), 8)

    def tile_waves(kx):
        wave_x = (2.0 * math.pi / NX) * (gy * WIDTH + kx).astype(F32)
        iy = gz * 8 + lax.broadcasted_iota(jnp.int32, (8, 128), 0)
        iz = lax.broadcasted_iota(jnp.int32, (8, 128), 1)
        wave_y = (2.0 * math.pi / NY) * jnp.where(iy < NY // 2, iy, iy - NY).astype(F32)
        wave_z = (2.0 * math.pi / NZ) * jnp.where(iz < NZ // 2, iz, iz - NZ).astype(F32)
        return wave_x, wave_y, wave_z

    loads[0].wait()
    loads[1].wait()

    @pl.loop(0, WIDTH)
    def _(kx):
        wave_x, wave_y, wave_z = tile_waves(kx)
        square = wave_x * wave_x + wave_y * wave_y + wave_z * wave_z
        inverse = jnp.where(square > 0, 1.0, 0.0) / jnp.where(square > 0, square, 1.0)
        first = octet(kx)
        scale = mask_ref[first, :].astype(F32) * jnp.where(gy * WIDTH + kx == 0, 1.0, 0.5)
        for c in range(2):
            at = octet(c * WIDTH + kx)
            v0, v1, v2 = cot_ref[0, at, :], cot_ref[1, at, :], cot_ref[2, at, :]
            along = (wave_x * v0 + wave_y * v1 + wave_z * v2) * inverse
            adj[0, at, :] = scale * (v0 - wave_x * along)
            adj[1, at, :] = scale * (v1 - wave_y * along)
            adj[2, at, :] = scale * (v2 - wave_z * along)

    def z_inverse(source, f, base):
        table = (zi_ref[0], zi_ref[1])
        view = sent.reshape(10, 1024, 128)
        for pair in range(4):
            wide = []
            for ky in (2 * pair, 2 * pair + 1):
                own = source[f, pl.ds(ky, 128, stride=8), :]
                wide.append(jnp.concatenate([own, jnp.concatenate([-own[64:], own[:64]], 0)], 1))
            done = three(table, halves(jnp.concatenate(wide, 0)), dot_nt)
            for k in range(2):
                at = pl.ds(2 * pair + k, 128, stride=8)
                view[base + f, at, :] = done[:128, k * 128 : k * 128 + 128]

                @pl.when(f < 2)
                def _():
                    view[base + 3 + f, at, :] = done[128:, k * 128 : k * 128 + 128]

    def flow_first(f):
        to_rings(lambda k: sent.at[f, k], ring.at[f, :, octet(z_lo), lanes(gy)], s1.at[f], r1.at[f])

    def flow_second(f):
        drain(ring.at[f], r1.at[f])
        to_sheets(lambda k: ring.at[f, k], plane.at[f, w], s2.at[f], r2.at[f])

    def pull_first(f):
        to_sheets(lambda k: sent.at[f, :, k], sheet.at[f - 4, w], s1.at[f], r1.at[f])

    def last_second():
        drain(sheet.at[0], r1.at[4])
        to_rings(lambda k: sheet.at[0, :, k], plane.at[4, :, octet(z_lo), lanes(gy)], s2.at[4], r2.at[4])

    def pull_second(f):
        @pl.when(kept_x)
        def _():
            drain_tiles(88, r1.at[f])
            for first, count in ((0, 4), (4 + 5 * z_lo, 3), (12, 4)):
                some = pl.ds(first, count)
                to_rings(
                    lambda k: sheet.at[f - 4, some, k], plane.at[f + 1, some, octet(z_lo), lanes(gy)],
                    s2.at[f], r2.at[f],
                )

    def send_visc():
        landing = visc.at[pl.ds(pl.multiple_of(gy * 64, 64), 64)]

        @pl.loop(1, 4)
        def _(step):
            other = (gy + step) % 4
            pltpu.make_async_remote_copy(
                src_ref=visc_ref.at[other], dst_ref=landing, send_sem=sv.at[0], recv_sem=rv.at[0],
                device_id={"gy": other, "gz": gz}, device_id_type=MESH,
            ).start()

        pltpu.make_async_copy(visc_ref.at[gy], landing, rv.at[0]).start()

    def pull_fields(f):
        pull_first(5 + f)

        @pl.when(f == 0)
        def _():
            pull_first(8)

        @pl.when(f == 2)
        def _():
            pull_first(9)

    loads[2].wait()

    @pl.when(kept)
    def _():
        z_inverse(adj, 0, 5)

    loads[3].wait()
    z_inverse(modes_ref, 0, 0)
    pl.semaphore_wait(barrier, RING + RINGS - 2)

    @pl.when(kept)
    def _():
        pull_fields(0)

    flow_first(0)
    @pl.loop(1, 3)
    def _(f):
        @pl.when(kept)
        def _():
            z_inverse(adj, f, 5)
            pull_fields(f)

        z_inverse(modes_ref, f, 0)

        @pl.when(f == 1)
        def _():
            flow_first(1)

    @pl.loop(6, 11)
    def _(slot):
        plane[slot, :, :, 384:] = jnp.zeros((RINGS, 16, 128), F32)
        plane[slot, 4:7, 8:, :384] = jnp.zeros((3, 8, 384), F32)
        plane[slot, 7:9, :, :384] = jnp.zeros((2, 16, 384), F32)
        plane[slot, 9:12, :8, :384] = jnp.zeros((3, 8, 384), F32)

    pull_second(5)
    pull_second(8)
    flow_second(0)
    pull_second(6)
    flow_first(2)
    for copy in loads[4:]:
        copy.wait()

    lane = lax.broadcasted_iota(jnp.int32, (1, NX), 1)
    wave_x = (2.0 * math.pi / NX) * ((lane // 128) * WIDTH + lane % WIDTH).astype(F32)
    sign = jnp.where(lane % 128 < WIDTH, -1.0, 1.0).astype(F32)

    def turn(value):
        parts = [pltpu.roll(value[:, k * 128 : k * 128 + 128], 64, 1) for k in range(value.shape[1] // 128)]
        return jnp.concatenate(parts, 1) * sign[:, : value.shape[1]]

    def wave_y_of(block):
        row = lax.broadcasted_iota(jnp.int32, (16, 1), 0)
        mode = (block // 4) * 64 + (block % 4) * 8 + (row // 8) * 32 + row % 8
        return (2.0 * math.pi / NY) * jnp.where(mode < NY // 2, mode, mode - NY).astype(F32)

    def curl(base, slots):
        @pl.loop(0, RINGS)
        def _(block):
            wave_y = wave_y_of(block)
            if 3 in slots:
                plane[base + 3, block] = plane[base + 3, block] - wave_x * turn(plane[base + 2, block])
            if 4 in slots:
                plane[base + 4, block] = wave_y * turn(plane[base + 2, block]) - plane[base + 4, block]
            if 5 in slots:
                plane[base + 5, block] = wave_x * turn(plane[base + 1, block]) - wave_y * turn(plane[base, block])

    half = NY // 2
    edge = lax.broadcasted_iota(jnp.int32, (half, 256), 0) == 0

    def to_cells(index):
        for h in range(2):
            cols = pl.ds(h * 256, 256)
            both = three((yi_ref[0], yi_ref[1]), halves(plane[index, :, :, cols].reshape(NY, 256)))
            top, low = both[:half], both[half:]
            spun = turn(low)
            rows[:half, cols] = jnp.where(edge, top, top + spun)
            rows[half:, cols] = jnp.where(edge, low, top - spun)
        moved = halves(rows[...])
        for h in range(2):
            cols = pl.ds(h * 256, 256)
            done = three(moved, (xi_ref[0, :, cols], xi_ref[1, :, cols]))
            phys[index, :, cols] = done

    count = thrust_ref.shape[1]
    turbine[...] = jnp.full((8, 128), -1000.0, F32)
    turbine[0:3, :count] = hub_ref[...].astype(F32)
    turbine[3:4, :count] = sector_ref[...].astype(F32)
    turbine[4:5, :count] = thrust_ref[...]
    hub_x, hub_y, hub_z, sector, thrust = [turbine[k : k + 1, :] for k in range(5)]
    normal_x = normal_y = jnp.zeros((1, 128), F32)
    for k in range(13):
        angle = (k - 6) * math.pi / 36.0
        normal_x = jnp.where(sector == float(k), math.cos(angle), normal_x)
        normal_y = jnp.where(sector == float(k), math.sin(angle), normal_y)
    cell_x = lax.broadcasted_iota(jnp.int32, (NX, 128), 0).astype(F32)
    hot = jnp.where(cell_x == hub_x, 1.0, 0.0).astype(BF16)
    cell_y = lax.broadcasted_iota(jnp.int32, (NY, 128), 0)
    cell_y = jnp.where(cell_y > half, NY + half - cell_y, cell_y)
    off_y = cell_y.astype(F32) - hub_y
    off_z = (gz * 4 + gy).astype(F32) - hub_z
    disk = jnp.where(off_y * off_y + off_z * off_z <= float(RADIUS * RADIUS), 1.0, 0.0)

    def project(first, inflow):
        def column(index, mean):
            high, low = halves(phys[index] + mean)
            return dot(high, hot) + dot(low, hot)

        mixed = normal_x * column(first, inflow[0]) + normal_y * column(first + 1, inflow[1])
        return jnp.sum(disk * mixed, axis=0, keepdims=True)

    @pl.loop(0, 9)
    def _(task):
        @pl.when(task == 0)
        def _():
            drain_tiles(66, r2.at[5])

        @pl.when(task == 1)
        def _():
            flow_second(1)
            pull_second(7)
            drain_tiles(66, r2.at[6])

        @pl.when(task == 2)
        def _():
            curl(6, (5,))

        @pl.when(task == 3)
        def _():
            pull_second(9)
            send_visc()
            flow_first(3)
            flow_second(2)
            pull_first(4)
            part[...] = jnp.zeros((8, 128), F32)
            part[1:2, :] = project(6, (0.0, 0.0))
            drain_tiles(66, r2.at[7])
            drain_tiles(66, r2.at[8])
            curl(6, (3,))

        @pl.when(task == 5)
        def _():
            drain(plane.at[0], r2.at[0])

        @pl.when(task == 6)
        def _():
            drain_tiles(66, r2.at[9])
            curl(6, (4,))

        @pl.when(task == 7)
        def _():
            drain(plane.at[1], r2.at[1])

        @pl.when(task == 8)
        def _():
            part[0:1, :] = project(0, (inflow_ref[0], inflow_ref[1]))
            to_rings(lambda k: part, part_a.at[e], sa.at[0], ra.at[0])
            drain(plane.at[2], r2.at[2])

        slot = jnp.int32(0)
        for step, value in enumerate((6, 7, 11, 9, 8, 0, 10, 1, 2)):
            slot = jnp.where(task == step, value, slot)
        to_cells(slot)

    flow_second(3)
    drain(visc, rv.at[0])
    first = lax.broadcasted_iota(jnp.int32, (half, half), 0)
    second = lax.broadcasted_iota(jnp.int32, (half, half), 1)
    swap = jnp.where((first + second) % half == 0, 1.0, 0.0).astype(BF16)
    high, low = halves(visc[half:])
    visc[half:] = dot(swap, high) + dot(swap, low)

    @pl.loop(0, 32)
    def _(block):
        at = octet(block)
        u0, u1, u2 = [phys[k, at] + inflow_ref[k] for k in range(3)]
        p0, p1, p2 = [phys[6 + k, at] for k in range(3)]
        q1, q0, q2 = [phys[9 + k, at] for k in range(3)]
        nu = visc[at]
        phys[9, at] = p1 * u2 - p2 * u1 - nu * q0
        phys[10, at] = p2 * u0 - p0 * u2 - nu * q1
        phys[11, at] = p0 * u1 - p1 * u0 - nu * q2

    def to_modes(source, target, extra=None):
        moved = halves(phys[source])
        for h in range(2):
            cols = pl.ds(h * 256, 256)
            spectrum = three(moved, (xf_ref[0, :, cols], xf_ref[1, :, cols]))
            top, low = spectrum[:half], spectrum[half:]
            even = jnp.where(edge, top, top + low)
            odd = jnp.where(edge, low, turn(low - top))
            done = three((yf_ref[0], yf_ref[1]), halves(jnp.concatenate([even, odd], 0)))
            if extra is not None:
                done = done + extra(cols)
            plane[target, :, :, cols] = done.reshape(RINGS, 16, 256)

    def mine(ref, k):
        return ref.at[:, octet(k // 4), lanes(k % 4)]

    def sheet_first(k, slot, at):
        to_sheets(lambda other: plane.at[slot, other], fold.at[at, w], s3.at[k], r3.at[k])

    def sheet_second(k, at):
        drain(fold.at[at], r3.at[k])
        to_rings(lambda other: mine(fold.at[at], other), pencil.at[k, e], s4.at[k], r4.at[k])

    def ring_first(k, slot, at):
        to_rings(lambda other: mine(plane.at[slot], other), turned.at[at, e], s3.at[k], r3.at[k])

    def ring_second(k, at):
        drain(turned.at[at], r3.at[k])
        to_sheets(lambda other: turned.at[at, :, other], pencil.at[k, :, w], s4.at[k], r4.at[k])

    @pl.loop(0, 3)
    def _(j):
        to_modes(9 + j, 6 + j)

        @pl.when(j == 0)
        def _():
            ring_first(0, 6, 0)
            drain(part_a, ra.at[0])
            total = part_a[0]
            for k in range(1, RING):
                total = total + part_a[k]
            part_b[RINGS] = total
            to_sheets(lambda k: part_b.at[RINGS], part_b.at[w], sa.at[1], ra.at[1])
            last_second()

        @pl.when(j == 1)
        def _():
            sheet_first(1, 7, 0)

    curl(0, (5,))
    to_cells(5)
    drain(part_b.at[pl.ds(0, RINGS)], ra.at[1])
    total = part_b[0]
    for k in range(1, RINGS):
        total = total + part_b[k]
    disk_speed = total[0:1] / disk_area()
    push = total[1:2]
    grad = -0.5 * SECTION_STEP * disk_speed * jnp.abs(disk_speed) * push
    grad_ref[...] = grad[:, : grad_ref.shape[1]]
    weight = -thrust * jnp.abs(disk_speed) * push / disk_area()

    for index, normal in ((9, normal_x), (10, normal_y)):
        high, low = halves(disk * (weight * normal))
        phys[index] = dot_nt(high, hot) + dot_nt(low, hot)

    drain(plane.at[3], r2.at[3])
    curl(0, (3,))
    to_cells(3)

    @pl.loop(0, 32)
    def _(block):
        at = octet(block)
        phys[9, at] = phys[9, at] + phys[3, at] * phys[8, at] - phys[5, at] * phys[7, at]

    ring_second(0, 0)
    spread_y = jnp.concatenate([wave_y_of(block) for block in range(RINGS)], 0)

    def spun(slot, cols):
        return turn(plane[slot, :, :, cols].reshape(NY, 256))

    def across(cols):
        return wave_x[:, cols.start : cols.start + 256]

    to_modes(9, 9, lambda cols: spread_y * spun(8, cols))
    ring_first(2, 9, 1)
    drain(plane.at[4], r2.at[4])
    curl(0, (4,))
    to_cells(4)

    @pl.loop(0, 32)
    def _(block):
        at = octet(block)
        w1, w0, w2 = [phys[3 + k, at] for k in range(3)]
        p0, p1, p2 = [phys[6 + k, at] for k in range(3)]
        phys[10, at] = phys[10, at] + w2 * p0 - w0 * p2
        phys[11, at] = w0 * p1 - w1 * p0

    to_modes(10, 10, lambda cols: -across(cols) * spun(8, cols))
    sheet_first(3, 10, 1)
    sheet_second(1, 0)
    to_modes(11, 11, lambda cols: across(cols) * spun(7, cols) - spread_y * spun(6, cols))
    sheet_first(4, 11, 2)
    ring_second(2, 1)
    sheet_second(3, 1)
    sheet_second(4, 2)
    pencils = pencil.reshape(5, 1024, 128)

    def z_forward(f, table, fields):
        for pair in range(4):
            tall = []
            for k in fields:
                own = jnp.concatenate([pencils[k, pl.ds(2 * pair + i, 128, stride=8), :] for i in range(2)], 1)
                tall += [own, turn(own)]
            done = three(table, halves(jnp.concatenate(tall, 0)))
            for i in range(2):
                at = pl.ds(2 * pair + i, 128, stride=8)
                doubled = jnp.where(
                    (lax.broadcasted_iota(jnp.int32, (128, 1), 0) % WIDTH == 0) & (gy == 0), 1.0, 2.0
                )
                result[f, at, :] = adj[f, at, :] * doubled + SECTION_STEP * done[:, i * 128 : i * 128 + 128].T

        pltpu.make_async_copy(result.at[f], out_ref.at[f], leave.at[f]).start()

    for k in range(3):
        drain(pencil.at[k], r4.at[k])
    z_forward(0, (zf_ref[0, 0], zf_ref[1, 0]), (2, 1))
    drain(pencil.at[3], r4.at[3])
    z_forward(1, (zf_ref[0, 1], zf_ref[1, 1]), (3, 0))
    drain(pencil.at[4], r4.at[4])
    z_forward(2, (zf_ref[0, 0, :, :256], zf_ref[1, 0, :, :256]), (4,))

    for f in range(4):
        drain_tiles(112, s1.at[f])
        drain_tiles(120, s2.at[f])
    drain_tiles(120, s1.at[4])
    drain_tiles(112, s2.at[4])
    for k in range(5):
        drain_tiles(112 if k in (0, 2) else 120, s3.at[k])
        drain_tiles(120 if k in (0, 2) else 112, s4.at[k])

    @pl.when(kept)
    def _():
        for f in range(5, 10):
            drain_tiles(120, s1.at[f])

    @pl.when(kept_x)
    def _():
        for f in range(5, 10):
            drain_tiles(77, s2.at[f])

    for f in range(3):
        pltpu.make_async_copy(result.at[f], out_ref.at[f], leave.at[f]).wait()
    drain(visc.at[pl.ds(0, 192)], sv.at[0])
    drain(part_a.at[pl.ds(0, RING - 1)], sa.at[0])
    drain(part_b.at[pl.ds(0, RINGS - 1)], sa.at[1])


def carry(adjoint, grad, adjoint_out, grad_out, rest, small, arrive, leave):
    pieces = [(adjoint.at[f, pl.ds(k * 512, 512)], rest.at[f, pl.ds(k * 512, 512)], adjoint_out.at[f, pl.ds(k * 512, 512)])
              for f in range(3) for k in range(2)]
    pieces.append((grad, small, grad_out))
    inward = [pltpu.make_async_copy(piece[0], piece[1], arrive.at[k]) for k, piece in enumerate(pieces)]
    outward = [pltpu.make_async_copy(piece[1], piece[2], leave.at[k]) for k, piece in enumerate(pieces)]
    for copy in inward:
        copy.start()
    for first, then in zip(inward, outward):
        first.wait()
        then.start()
    for copy in outward:
        copy.wait()


def local(velocity_hat, inflow, viscosity, cot_hat, mode_mask, hub_cells, yaw_sector, thrust):
    count = thrust.shape[0]
    vmem = pl.BlockSpec(memory_space=pltpu.VMEM)
    smem = pl.BlockSpec(memory_space=pltpu.SMEM)
    dma = pltpu.SemaphoreType.DMA
    z_inverse, z_forward, y_inverse, y_forward, x_inverse, x_forward = [jnp.asarray(t) for t in tables()]
    operands = [
        cot_hat.reshape(3, 1024, 128), mode_mask.reshape(512, 128), z_inverse, velocity_hat.reshape(3, 1024, 128),
        y_inverse, x_inverse, x_forward, y_forward, z_forward,
    ]
    adjoint, grad = pl.pallas_call(
        kernel,
        out_shape=(
            jax.ShapeDtypeStruct((3, 1024, 128), F32),
            jax.ShapeDtypeStruct((1, count), F32),
        ),
        in_specs=[smem, vmem, vmem, vmem] + [pl.BlockSpec(memory_space=pl.ANY)] * 10,
        out_specs=(pl.BlockSpec(memory_space=pl.ANY), vmem),
        scratch_shapes=[pltpu.VMEM(each.shape, each.dtype) for each in operands] + [
            pltpu.VMEM((3, 1024, 128), F32),
            pltpu.VMEM((10, RING, RINGS, 8, 128), F32),
            pltpu.VMEM((4, RINGS, 16, NX), F32),
            pltpu.VMEM((6, RINGS, RING, 8, 128), F32),
            pltpu.VMEM((12, RINGS, 16, NX), F32),
            pltpu.VMEM((12, NY, NX), F32),
            pltpu.VMEM((NY, NX), F32),
            pltpu.VMEM((NY, NX), F32),
            pltpu.VMEM((3, RINGS, 16, NX), F32),
            pltpu.VMEM((2, RING, RINGS, 8, 128), F32),
            pltpu.VMEM((5, RING, RINGS, 8, 128), F32),
            pltpu.VMEM((3, 1024, 128), F32),
            pltpu.VMEM((8, 128), F32),
            pltpu.VMEM((RING, 8, 128), F32),
            pltpu.VMEM((RINGS + 1, 8, 128), F32),
            pltpu.VMEM((8, 128), F32),
            dma((10,)), dma((10,)), dma((10,)), dma((10,)),
            dma((5,)), dma((5,)), dma((5,)), dma((5,)),
            dma((1,)), dma((1,)), dma((2,)), dma((2,)), dma((9,)), dma((3,)),
        ],
        compiler_params=pltpu.CompilerParams(
            collective_id=0, has_side_effects=True, vmem_limit_bytes=60 * 1024 * 1024
        ),
    )(
        inflow,
        hub_cells.T,
        yaw_sector.reshape(1, count),
        thrust.reshape(1, count),
        viscosity,
        *operands,
    )
    whole = pl.BlockSpec(memory_space=pl.ANY)
    adjoint, grad = pl.pallas_call(
        carry,
        out_shape=tuple(jax.ShapeDtypeStruct(each.shape, F32) for each in (adjoint, grad)),
        in_specs=[whole, whole],
        out_specs=(whole, whole),
        scratch_shapes=[pltpu.VMEM(adjoint.shape, F32), pltpu.VMEM(grad.shape, F32), dma((7,)), dma((7,))],
    )(adjoint, grad)
    return adjoint.reshape(velocity_hat.shape), grad.reshape(count)


def solution(mesh):
    placed = (
        P(None, None, "gy", "gz", None),
        P(),
        P("gz", "gy", None),
        P(None, None, "gy", "gz", None),
        P("gy", "gz", None),
        P(),
        P(),
        P(),
    )
    return jax.shard_map(
        local,
        mesh=mesh,
        in_specs=placed,
        out_specs=(P(None, None, "gy", "gz", None), P()),
        check_vma=False,
    )
```
